256 devices in a mesh: pp: 8 (over y_hi, x), dp: 8 (over z), tp: 4 (over y_lo, core).
Axes of the slice: x: 4, y: 4 (y_hi: 2, y_lo: 2; y = y_hi * 2 + y_lo), z: 8, core: 2. Of those that a mesh axis runs over, the one named last changes fastest.
Arguments:
- hidden: bfloat16 [256, 128, 8192], P(('pp', 'dp'), None, 'tp'), may hold values from -6 to 6
- positions: int32 [256, 8], P(('pp', 'dp')), may hold values from 0 to 127, as said below
- image_tokens: int32 [256], P(('pp', 'dp')), may hold values from 1 to 8, as said below
- groups: int32 [256, 1], P(('pp', 'dp')), may hold values from 0 to 7; in each aligned block of 4 rows (0 to 3, 4 to 7, ...) at most 2 rows name the same one
- latents: bfloat16 [256, 8, 1536], P(('pp', 'dp')), may hold values from -6 to 6
- out_grad: bfloat16 [256, 8, 1536], P(('pp', 'dp'), None, 'tp'), may hold values from -6 to 6
- w_conn: bfloat16 [1536, 8192], P(None, 'tp'), may hold values from -0.0625 to 0.0625
- w_mod: bfloat16 [1536, 3, 1536], P(('pp', 'dp'), None, 'tp'), may hold values from -0.15625 to 0.15625
- w_up: bfloat16 [8, 1536, 6144], P('dp', 'pp', 'tp'), may hold values from -0.15625 to 0.15625
- w_down: bfloat16 [8, 1536, 6144], P('dp', 'pp', 'tp'), may hold values from -0.078125 to 0.078125
Outputs:
- generated: bfloat16 [256, 8, 1536], P(('pp', 'dp'), None, 'tp')
- row_grad: bfloat16 [256, 8, 8192], P(('pp', 'dp'), None, 'tp')
- conn_grad: float32 [1536, 8192], P(('pp', 'dp'), 'tp')
The draws below stay inside these ranges and needn't reach their ends.
Inputs may be any that keep to these rules, and one draw needn't show every extreme that they name: Each sample's 8 positions are distinct and increasing. `image_tokens`: the first sample of each aligned block of 4 samples uses all 8. `groups`: within the rows of one device (aligned blocks of 4) no group is named more than 2 times.
All inputs are finite; a program needn't handle non-finite values.
Results may differ from the reference program's by a relative error of at most 0.034.
Values may be sent and summed in bfloat16 or wider, within the bound.
A program may use at most 128 MiB of HBM per device.

```python
import math
import jax
import jax.numpy as jnp
import numpy as np
from jax import lax

D = 8192
C = 1536
FF = 6144
CAP = 2
SAMP_DEV = 4
SEQ = 128
IMG = 8
SAMPLES = 256
N_DP = 8


def draw_positions(key, part):
    key = jax.random.fold_in(key, 11)
    sample_keys = jax.random.split(key, SAMPLES)

    def one_sample(sample_key):
        shuffled = jax.random.permutation(sample_key, SEQ)
        return jnp.sort(shuffled[:IMG])
    return jax.vmap(one_sample)(sample_keys).astype(jnp.int32)


def draw_image_tokens(key, part):
    key = jax.random.fold_in(key, 23)
    counts = jax.random.randint(key, (SAMPLES,), 1, IMG + 1)
    leading = jnp.arange(SAMPLES) % SAMP_DEV == 0
    return jnp.where(leading, IMG, counts).astype(jnp.int32)


def levels(stream_key, extent, cuts, low, top_value):
    def one(axis_at, blocks):
        steps = jax.random.uniform(jax.random.fold_in(jax.random.fold_in(stream_key, 6), axis_at), (blocks,), jnp.float32, low / len(cuts), top_value / len(cuts))
        return jnp.repeat(jnp.exp(steps), extent[axis_at] // blocks).reshape((-1,) + (1,) * (len(extent) - axis_at - 1))

    factor_of = one(*cuts[0])
    for cut in cuts[1:]:
        factor_of = factor_of * one(*cut)
    return factor_of


def shared_out(rng, own, number, rows, amount, top, most, skew):
    order = jax.random.permutation(rng, amount)
    packed, ordinary = load_shares(amount, rows * top, most, skew, True), load_shares(amount, rows * top, most, skew, False)
    places = jnp.arange(amount)

    def named(sizes, offset_by):
        used = int((sizes > 0).sum())
        fixed = max(1, used // 4)
        passed = fixed + (places - fixed + offset_by * (used - fixed)) % max(1, amount - fixed)
        return jnp.zeros((amount,), jnp.int32).at[order[jnp.where(places < fixed, places, passed)]].set(jnp.asarray(sizes, jnp.int32))

    sizes = jnp.where(number % 4 == 0, named(packed, number // 4), named(ordinary, number - number // 4 - 1))
    mixed = jax.random.permutation(jax.random.fold_in(own, 3), amount)
    donor, taker = mixed[0:amount // 2 * 2:2], mixed[1:amount // 2 * 2:2]
    room = jnp.minimum(sizes[donor] - 1, most - sizes[taker]) // 2
    room = jnp.where((donor == order[0]) | (taker == order[0]) | (sizes[taker] == 0), 0, jnp.maximum(room, 0))
    passed = jax.random.randint(jax.random.fold_in(own, 4), (amount // 2,), 0, 1 << 20) % (room + 1)
    sizes = sizes.at[donor].add(-passed).at[taker].add(passed)
    labels = jnp.searchsorted(jnp.cumsum(sizes), jnp.arange(rows * top), side="right").astype(jnp.int32)
    listing = labels.reshape(top, rows).T
    listing = listing[jax.random.permutation(jax.random.fold_in(own, 1), rows)]
    offset_by = jax.random.randint(jax.random.fold_in(own, 2), (rows, 1), 0, top)
    return jnp.take_along_axis(listing, (jnp.arange(top)[None, :] + offset_by) % top, axis=1)


def load_shares(amount, total, reach, lean, full):
    portions = [(1 << 20) // math.isqrt(grade ** lean) + 1 for grade in range(1, amount + 1)]
    largest = reach if full else min(reach, max(-(-total // amount), total * portions[0] // sum(portions)))
    least = 1 if total - largest >= amount - 1 else 0
    given, rest = [largest] + [least] * (amount - 1), total - largest - least * (amount - 1)
    while rest > 0:
        movable = [i for i in range(1, amount) if given[i] < largest] or [i for i in range(1, amount) if given[i] < reach]
        whole, remaining = sum([portions[i] for i in movable]), rest
        for i in movable:
            extra = min(reach - given[i], max(1, remaining * portions[i] // whole), rest)
            given[i] = given[i] + extra
            rest = rest - extra
    return np.array(given)


def normal_values(key, dims, deviation, limit, cuts=(), held_as=jnp.bfloat16):
    values = jax.random.normal(key, dims, jnp.float32) * deviation
    if len(cuts) > 0:
        values = levels(key, dims, cuts, -0.22, 0.18) * values
    return jnp.clip(values, min=-limit, max=limit).astype(held_as)


def setup_inputs(seed: int = 0) -> dict:
    key_list = jax.random.split(jax.random.key(seed), 11)
    hidden = normal_values(key_list[0], (SAMPLES, SEQ, D), 1.0, 6.0, ((0, 64), (2, 4)))
    positions = draw_positions(jax.random.fold_in(key_list[10], 71), 0)
    image_tokens = draw_image_tokens(jax.random.fold_in(key_list[10], 71), 0)
    groups_keys = jax.random.split(jax.random.fold_in(key_list[3], 1), SAMPLES // SAMP_DEV)
    groups_turns = jax.random.permutation(jax.random.fold_in(key_list[3], 3), SAMPLES // SAMP_DEV)
    groups = jax.vmap(lambda own, number: shared_out(jax.random.fold_in(key_list[3], 2), own, number, SAMP_DEV, N_DP, 1, CAP, 2))(groups_keys, groups_turns).reshape((SAMPLES, 1))
    latents = normal_values(key_list[4], (SAMPLES, IMG, C), 1.0, 6.0, ((0, 64),))
    out_grad = normal_values(key_list[5], (SAMPLES, IMG, C), 1.0, 6.0, ((0, 64), (2, 4)))
    w_conn = normal_values(key_list[6], (C, D), D ** -0.5, 0.0625, ((1, 4),))
    w_mod = normal_values(key_list[7], (C, 3, C), C ** -0.5, 0.15625, ((0, 64), (2, 4)))
    w_up = normal_values(key_list[8], (N_DP, C, FF), C ** -0.5, 0.15625, ((0, 8), (1, 8), (2, 4)))
    w_down = normal_values(key_list[9], (N_DP, C, FF), FF ** -0.5, 0.078125, ((0, 8), (1, 8), (2, 4)))
    return {"hidden": hidden, "positions": positions, "image_tokens": image_tokens, "groups": groups, "latents": latents, "out_grad": out_grad, "w_conn": w_conn, "w_mod": w_mod, "w_up": w_up, "w_down": w_down}


tanh_coef = 0.7978845608028654
cubic_term = 0.044715

def gelu_pair(preact):
    inner_arg = tanh_coef * (preact + cubic_term * preact * preact * preact)
    tanh_value = jnp.tanh(inner_arg)
    gelu_value = 0.5 * preact * (1.0 + tanh_value)
    gelu_slope = 0.5 * (1.0 + tanh_value) + 0.5 * preact * (1.0 - tanh_value * tanh_value) * tanh_coef * (1.0 + 3.0 * cubic_term * preact * preact)
    return (gelu_value, gelu_slope)

def normalize(latent):
    average = lax.optimization_barrier(jnp.mean(latent, axis=-1, keepdims=True))
    centered = latent - average
    variance = lax.optimization_barrier(jnp.mean(centered * centered, axis=-1, keepdims=True))
    return centered / jnp.sqrt(variance + 1e-06)

def reference(hidden, positions, image_tokens, groups, latents, out_grad, w_conn, w_mod, w_up, w_down):
    cond_width = w_conn.shape[0]
    row_depth = w_conn.shape[1]
    sample_total = hidden.shape[0]
    picked = jnp.take_along_axis(hidden, positions[:, :, None].astype(jnp.int32), axis=1)
    flat_rows = picked.reshape(-1, row_depth)
    valid_mask = (jnp.arange(IMG)[None, :] < image_tokens[:, None]).astype(jnp.float32).reshape(-1, 1)
    condition = jnp.dot(flat_rows, w_conn.T, preferred_element_type=jnp.float32).astype(jnp.bfloat16)
    modulation = jnp.dot(condition, w_mod.reshape(cond_width, 3 * cond_width), preferred_element_type=jnp.float32).reshape(-1, 3, cond_width)
    shift_part = modulation[:, 0]
    scale_part = modulation[:, 1]
    gate_part = modulation[:, 2]
    latent = latents.reshape(-1, cond_width).astype(jnp.float32)
    normed = normalize(latent)
    h_in = (normed * (1.0 + scale_part) + shift_part).astype(jnp.bfloat16)
    cotangent = out_grad.reshape(-1, cond_width).astype(jnp.float32)
    d_out = (gate_part * cotangent).astype(jnp.bfloat16)

    def per_sample(sample_inputs):
        sample_hidden, sample_grad, group_id = sample_inputs
        up_matrix = w_up[group_id]
        down_matrix = w_down[group_id]
        preact = jnp.dot(sample_hidden, up_matrix, preferred_element_type=jnp.float32)
        gelu_value, gelu_slope = gelu_pair(preact)
        activation = gelu_value.astype(jnp.bfloat16)
        ff_sample = jnp.dot(activation, down_matrix.T, preferred_element_type=jnp.float32)
        d_act = jnp.dot(sample_grad, down_matrix, preferred_element_type=jnp.float32)
        d_pre = (d_act * gelu_slope).astype(jnp.bfloat16)
        d_hin_sample = jnp.dot(d_pre, up_matrix.T, preferred_element_type=jnp.float32)
        return (ff_sample, d_hin_sample)
    ff_out, d_hin = lax.map(per_sample, (h_in.reshape(sample_total, IMG, cond_width), d_out.reshape(sample_total, IMG, cond_width), groups[:, 0].astype(jnp.int32)))
    ff_out = ff_out.reshape(-1, cond_width)
    d_hin = d_hin.reshape(-1, cond_width)
    generated = (valid_mask * (latent + gate_part * ff_out)).astype(jnp.bfloat16).reshape(sample_total, IMG, cond_width)
    d_mod = jnp.stack([d_hin, d_hin * normed, cotangent * ff_out], axis=1).astype(jnp.bfloat16)
    d_cond = (valid_mask * jnp.dot(d_mod.reshape(-1, 3 * cond_width), w_mod.reshape(cond_width, 3 * cond_width).T, preferred_element_type=jnp.float32)).astype(jnp.bfloat16)
    row_grad = jnp.dot(d_cond, w_conn, preferred_element_type=jnp.float32).astype(jnp.bfloat16).reshape(sample_total, IMG, row_depth)
    conn_grad = jnp.dot(d_cond.T, flat_rows, preferred_element_type=jnp.float32) / (SAMPLES // SAMP_DEV)
    return (generated, row_grad, conn_grad)
```

```python
import functools

import jax
import jax.numpy as jnp
from jax import lax
from jax.experimental import pallas as pl
from jax.experimental.pallas import tpu as pltpu
from jax.sharding import PartitionSpec as P

MESH = pl.DeviceIdType.MESH
CAP = 2
F32 = jnp.float32
BF16 = jnp.bfloat16
tanh_coef = 0.7978845608028654
cubic_term = 0.044715


def gelu_pair(preact):
    inner_arg = tanh_coef * (preact + cubic_term * preact * preact * preact)
    tanh_value = jnp.tanh(inner_arg)
    gelu_value = 0.5 * preact * (1.0 + tanh_value)
    gelu_slope = 0.5 * (1.0 + tanh_value) + 0.5 * preact * (
        1.0 - tanh_value * tanh_value
    ) * tanh_coef * (1.0 + 3.0 * cubic_term * preact * preact)
    return (gelu_value, gelu_slope)


def dot_nn(a, b):
    return lax.dot_general(a, b, (((1,), (0,)), ((), ())), preferred_element_type=F32)


def dot_nt(a, b):
    return lax.dot_general(a, b, (((1,), (1,)), ((), ())), preferred_element_type=F32)


def kernel(
    groups, tokens, positions, hidden, latents, out_grad, w_conn, w_mod, w_up, w_down,
    gen_o, row_o, conn_o,
    hid, wc, wu, wd, wm, pick, pkg,
    cps, cpr, cbz, cz, mps, mrs,
    slot, hd, slope_s, ffs, rff, dhs, rdh, rets, ret,
    rdm, dcs, dcr, dcz, dch, cgs, rcg,
    lsem, ssem, rsem,
):
    p, z, t = lax.axis_index("pp"), lax.axis_index("dp"), lax.axis_index("tp")
    yh, x = p // 4, lax.rem(p, 4)
    m = yh * 4 + t
    rows = 32

    def zdev(d):
        return (p, lax.rem(z + d + 8, 8), t)

    def pdev(d):
        return (lax.rem(p + d, 8), z, t)

    def tdev(e):
        return (p, z, lax.rem(t + e, 4))

    def mdev(e):
        mm = lax.rem(m + e, 8)
        return ((mm // 4) * 4 + x, z, lax.rem(mm, 4))

    loc = []

    def load(src, dst):
        c = pltpu.make_async_copy(src, dst, lsem.at[len(loc)])
        c.start()
        loc.append(c)
        return c

    c_hid = load(hidden, hid)
    c_wc = [
        load(w_conn.at[pl.ds(512 * i, 512)], wc.at[pl.ds(512 * i, 512)]) for i in range(3)
    ]

    barrier = pltpu.get_barrier_semaphore()
    peers = [zdev(d) for d in range(1, 8)]
    peers += [pdev(d) for d in (1, 2, 3, 5, 6, 7)]
    peers += [mdev(e) for e in range(1, 8)]
    for dev in peers:
        pl.semaphore_signal(barrier, inc=1, device_id=dev, device_id_type=MESH)
    pl.semaphore_wait(barrier, len(peers))

    sent = []

    def send(src, dst, dev):
        k = len(sent)
        c = pltpu.make_async_remote_copy(
            src_ref=src, dst_ref=dst, send_sem=ssem.at[k], recv_sem=rsem.at[k],
            device_id=dev, device_id_type=MESH,
        )
        c.start()
        sent.append(c)
        return c

    def arrive(copies):
        for c in copies:
            c.wait_recv()

    wm[p] = w_mod[...]
    r_wm = [send(w_mod, wm.at[p], pdev(d)) for d in range(1, 8)]

    own_rows = pl.ds(pl.multiple_of(192 * p, 192), 192)

    def half(ref, which):
        return ref.at[0, :, pl.ds(pl.multiple_of(768 * which, 768), 768)]

    def spread(src, dst):
        out = []
        for d in range(1, 8):
            dev = pdev(d)
            out.append(send(half(src, dev[0] // 4), dst.at[own_rows], dev))
        return out

    c_wu = load(half(w_up, yh), wu.at[own_rows])
    c_wd = load(half(w_down, yh), wd.at[own_rows])
    r_wu = spread(w_up, wu)
    r_wd = spread(w_down, wd)

    seq_iota = lax.broadcasted_iota(jnp.int32, (8, 128), 1)
    row_iota = lax.broadcasted_iota(jnp.int32, (8, 128), 0)
    c_hid.wait()
    parts = []
    for s in range(4):
        at = jnp.zeros((8, 128), jnp.int32)
        for i in range(8):
            at = jnp.where(row_iota == i, positions[s, i], at)
        sel = jnp.where(seq_iota == at, 1.0, 0.0).astype(BF16)
        parts.append(dot_nn(sel, hid[s]))
    pick[...] = jnp.concatenate(parts, axis=0).astype(BF16)
    pkg[0] = pick[...]

    for i in range(3):
        c_wc[i].wait()
        part = dot_nt(pick[...], wc[pl.ds(512 * i, 512), :])
        cps[:, pl.ds(512 * i, 512)] = part.astype(BF16)
    r_cp = [send(cps, cpr.at[e - 1], tdev(e)) for e in range(1, 4)]

    lat = latents[...].astype(F32).reshape(rows, 1536)
    mean = jnp.mean(lat, axis=-1, keepdims=True)
    cent = lat - mean
    var = jnp.mean(cent * cent, axis=-1, keepdims=True)
    inv = 1.0 / jnp.sqrt(var + 1e-06)
    mine = pl.ds(pl.multiple_of(t * 384, 384), 384)
    lat_t = latents[:, :, mine].astype(F32).reshape(rows, 384)
    normed = (lat_t - mean) * inv
    cot = out_grad[...].astype(F32).reshape(rows, 384)

    gs = [groups[s, 0] for s in range(4)]
    places = []
    for s in range(4):
        rank = 0
        for q in range(s):
            rank = rank + jnp.where(gs[q] == gs[s], 1, 0)
        places.append(gs[s] * CAP + rank)
    big_r = lax.broadcasted_iota(jnp.int32, (128, rows), 0)
    big_c = lax.broadcasted_iota(jnp.int32, (128, rows), 1)
    place = jnp.zeros((128, rows), jnp.int32)
    for s in range(4):
        place = jnp.where(big_c // 8 == s, places[s], place)
    onehot = jnp.where(big_r == place * 8 + lax.rem(big_c, 8), 1.0, 0.0).astype(BF16)
    flip_r = lax.broadcasted_iota(jnp.int32, (rows, 128), 0)
    flip_c = lax.broadcasted_iota(jnp.int32, (rows, 128), 1)
    place_f = jnp.zeros((rows, 128), jnp.int32)
    for s in range(4):
        place_f = jnp.where(flip_r // 8 == s, places[s], place_f)
    onehot_f = jnp.where(flip_c == place_f * 8 + lax.rem(flip_r, 8), 1.0, 0.0).astype(BF16)
    one_r = lax.broadcasted_iota(jnp.int32, (rows, 384), 0)
    used = jnp.zeros((rows, 384), jnp.int32)
    for s in range(4):
        used = jnp.where(one_r // 8 == s, tokens[s], used)
    valid = jnp.where(lax.rem(one_r, 8) < used, 1.0, 0.0)

    arrive(r_cp)
    cond = cps[...].astype(F32)
    for e in range(3):
        cond = cond + cpr[e].astype(F32)
    cond = cond.astype(BF16).astype(F32).T
    gap = jnp.zeros((8, rows), F32)
    pieces = []
    for zz in range(8):
        for pp in range(8):
            pieces.append(cond[24 * (8 * pp + zz) : 24 * (8 * pp + zz) + 24])
            pieces.append(gap)
    cond = jnp.concatenate(pieces, axis=0).T.astype(BF16)
    for zz in range(8):
        cbz[zz] = cond[:, 256 * zz : 256 * zz + 256]
    r_cz = []
    for d in range(1, 8):
        dev = zdev(d)
        r_cz.append(send(cbz.at[dev[1]], cz.at[d], dev))
    cz[0] = cbz[z]

    arrive(r_wm)
    wmod = wm[...].reshape(256, 1152)
    r_mr = []
    arrive(r_cz)
    pooled = cz[...].reshape(256, 256)
    mod_all = dot_nn(pooled, wmod).astype(BF16).reshape(8, rows, 1152)
    mps[...] = mod_all
    for d in (4, 3, 5, 2, 6, 1, 7):
        r_mr.append(send(mps.at[d], mrs.at[d], zdev(-d)))
    mod = mps[0].astype(F32)
    arrive(r_mr)
    for d in range(1, 8):
        mod = mod + mrs[d].astype(F32)
    shift, scale, gate = mod[:, :384], mod[:, 384:768], mod[:, 768:]

    h_in = (normed * (1.0 + scale) + shift).astype(BF16)
    d_out = (gate * cot).astype(BF16)
    packed = dot_nn(onehot, jnp.concatenate([h_in, d_out], axis=1)).astype(BF16)
    slot[...] = packed.reshape(8, 16, 768)
    r_sl = []
    for d in range(1, 8):
        dev = zdev(d)
        r_sl.append(send(slot.at[dev[1]], hd.at[m, pl.ds(16 * d, 16)], dev))
    hd[m, pl.ds(0, 16)] = slot[z]
    arrive(r_sl)
    r_h = [send(hd.at[m, :, pl.ds(0, 384)], hd.at[m, :, pl.ds(0, 384)], mdev(e)) for e in range(1, 8)]
    r_d = [send(hd.at[m, :, pl.ds(384, 384)], hd.at[m, :, pl.ds(384, 384)], mdev(e)) for e in range(1, 8)]
    r_pk = [send(pick, pkg.at[d], zdev(d)) for d in range(1, 8)]

    c_wu.wait()
    arrive(r_wu)
    arrive(r_h)

    def both(k, lo):
        return jnp.concatenate([hd[k, :, lo : lo + 384], hd[4 + k, :, lo : lo + 384]], axis=0)

    pre = dot_nn(both(0, 0), wu[0:384, :])
    for k in range(1, 4):
        pre = pre + dot_nn(both(k, 0), wu[384 * k : 384 * k + 384, :])
    value, slope = gelu_pair(pre)
    act = value.astype(BF16)
    slope_s[...] = slope
    c_wd.wait()
    arrive(r_wd)
    for k in range(4):
        ff = dot_nt(act, wd[384 * k : 384 * k + 384, :]).astype(BF16)
        ffs[k] = ff[:128]
        ffs[4 + k] = ff[128:]
    r_ff = []
    for e in range(1, 8):
        r_ff.append(send(ffs.at[lax.rem(m + e, 8)], rff.at[e - 1], mdev(e)))
    arrive(r_d)
    d_act = dot_nn(both(0, 384), wd[0:384, :])
    for k in range(1, 4):
        d_act = d_act + dot_nn(both(k, 384), wd[384 * k : 384 * k + 384, :])
    d_pre = (d_act * slope_s[...]).astype(BF16)
    for k in range(4):
        dh = dot_nt(d_pre, wu[384 * k : 384 * k + 384, :]).astype(BF16)
        dhs[k] = dh[:128]
        dhs[4 + k] = dh[128:]
    r_dh = []
    for e in range(1, 8):
        r_dh.append(send(dhs.at[lax.rem(m + e, 8)], rdh.at[e - 1], mdev(e)))
    arrive(r_ff)
    total = ffs[m].astype(F32)
    for e in range(7):
        total = total + rff[e].astype(F32)
    rets[:, :, pl.ds(0, 384)] = total.astype(BF16).reshape(8, 16, 384)
    arrive(r_dh)
    total = dhs[m].astype(F32)
    for e in range(7):
        total = total + rdh[e].astype(F32)
    rets[:, :, pl.ds(384, 384)] = total.astype(BF16).reshape(8, 16, 384)
    r_rt = [send(rets.at[d], ret.at[z], zdev(-d)) for d in range(1, 8)]
    ret[z] = rets[0]
    arrive(r_rt)
    home = dot_nn(onehot_f, ret[...].reshape(128, 768))
    ff_out, d_hin = home[:, :384], home[:, 384:]
    gen_o[...] = (valid * (lat_t + gate * ff_out)).reshape(4, 8, 384).astype(BF16)
    d_mod = jnp.concatenate(
        [valid * d_hin, valid * (d_hin * normed), valid * (cot * ff_out)], axis=1
    )
    rdm[0] = d_mod.astype(BF16)
    r_dm = [send(rdm.at[0], rdm.at[d], zdev(d)) for d in (4, 3, 5, 2, 6, 1, 7)]
    arrive(r_dm)
    dcs[...] = dot_nt(rdm[...].reshape(256, 1152), wm[...].reshape(256, 1152)).astype(BF16)
    r_dc = [send(dcs, dcr.at[e - 1], tdev(e)) for e in range(1, 4)]
    arrive(r_dc)
    d_cond = dcs[...].astype(F32)
    for e in range(3):
        d_cond = d_cond + dcr[e].astype(F32)
    d_cond = d_cond.astype(BF16)
    dcz[...] = d_cond.reshape(8, rows, 256)
    r_dz = [send(dcz.at[d], dch.at[z], zdev(-d)) for d in range(1, 8)]
    dch[z] = dcz[0]

    arrive(r_pk)
    turned = d_cond.astype(F32).T.astype(BF16)
    for i in range(4):
        cols = pl.ds(512 * i, 512)
        cg = dot_nn(turned, pkg[:, :, cols].reshape(256, 512))
        cgs[:, :, cols] = cg.astype(BF16).reshape(8, 32, 512)
    r_cg = []
    for d in range(1, 8):
        dev = pdev(d)
        r_cg.append(send(cgs.at[dev[0]], rcg.at[d - 1], dev))

    arrive(r_dz)
    back = jnp.concatenate([dch[zz].astype(F32) for zz in range(8)], axis=1).T
    pieces = []
    for pp in range(8):
        for zz in range(8):
            pieces.append(back[256 * zz + 32 * pp : 256 * zz + 32 * pp + 24])
    back = jnp.concatenate(pieces, axis=0).T.astype(BF16)
    for i in range(4):
        cols = pl.ds(512 * i, 512)
        row_o[:, :, cols] = dot_nn(back, wc[:, cols]).reshape(4, 8, 512).astype(BF16)

    arrive(r_cg)
    for i in range(4):
        cols = pl.ds(512 * i, 512)
        cg = cgs[p, :, cols].astype(F32)
        for e in range(7):
            cg = cg + rcg[e, :, cols].astype(F32)
        conn_o[:, cols] = cg[:24] * (1.0 / 64.0)
    for c in sent:
        c.wait_send()


def local(hidden, positions, image_tokens, groups, latents, out_grad, w_conn, w_mod, w_up, w_down):
    w_mod2 = jnp.pad(w_mod.reshape(24, 1152), ((0, 8), (0, 0)))
    vm = pl.BlockSpec(memory_space=pltpu.VMEM)
    sm = pl.BlockSpec(memory_space=pltpu.SMEM)
    hb = pl.BlockSpec(memory_space=pl.ANY)
    V = pltpu.VMEM
    n_copies = 7 * 14 + 7 + 3 * 2 + 7
    return pl.pallas_call(
        kernel,
        out_shape=(
            jax.ShapeDtypeStruct((4, 8, 384), BF16),
            jax.ShapeDtypeStruct((4, 8, 2048), BF16),
            jax.ShapeDtypeStruct((24, 2048), F32),
        ),
        in_specs=[sm, sm, sm, hb, vm, vm, hb, vm, hb, hb],
        out_specs=(vm, vm, vm),
        scratch_shapes=[
            V((4, 128, 2048), BF16),
            V((1536, 2048), BF16),
            V((1536, 768), BF16),
            V((1536, 768), BF16),
            V((8, 32, 1152), BF16),
            V((32, 2048), BF16),
            V((8, 32, 2048), BF16),
            V((32, 1536), BF16),
            V((3, 32, 1536), BF16),
            V((8, 32, 256), BF16),
            V((8, 32, 256), BF16),
            V((8, 32, 1152), BF16),
            V((8, 32, 1152), BF16),
            V((8, 16, 768), BF16),
            V((8, 128, 768), BF16),
            V((256, 768), F32),
            V((8, 128, 384), BF16),
            V((7, 128, 384), BF16),
            V((8, 128, 384), BF16),
            V((7, 128, 384), BF16),
            V((8, 16, 768), BF16),
            V((8, 16, 768), BF16),
            V((8, 32, 1152), BF16),
            V((256, 256), BF16),
            V((3, 256, 256), BF16),
            V((8, 32, 256), BF16),
            V((8, 32, 256), BF16),
            V((8, 32, 2048), BF16),
            V((7, 32, 2048), BF16),
            pltpu.SemaphoreType.DMA((8,)),
            pltpu.SemaphoreType.DMA((n_copies,)),
            pltpu.SemaphoreType.DMA((n_copies,)),
        ],
        compiler_params=pltpu.CompilerParams(
            collective_id=0, has_side_effects=True, vmem_limit_bytes=56 * 2**20
        ),
        cost_estimate=pl.CostEstimate(
            flops=6_000_000_000, bytes_accessed=16_000_000, transcendentals=200_000
        ),
    )(groups, image_tokens, positions, hidden, latents, out_grad, w_conn, w_mod2, w_up, w_down)


def solution(mesh):
    placed = (
        P(("pp", "dp"), None, "tp"),
        P(("pp", "dp"), None),
        P(("pp", "dp")),
        P(("pp", "dp"), None),
        P(("pp", "dp"), None, None),
        P(("pp", "dp"), None, "tp"),
        P(None, "tp"),
        P(("pp", "dp"), None, "tp"),
        P("dp", "pp", "tp"),
        P("dp", "pp", "tp"),
    )
    return jax.shard_map(
        local,
        mesh=mesh,
        in_specs=placed,
        out_specs=(P(("pp", "dp"), None, "tp"), P(("pp", "dp"), None, "tp"), P(("pp", "dp"), "tp")),
        check_vma=False,
    )
```

```python
import functools

import jax
import jax.numpy as jnp
from jax import lax
from jax.experimental import pallas as pl
from jax.experimental.pallas import tpu as pltpu
from jax.sharding import PartitionSpec as P

MESH = pl.DeviceIdType.MESH
CAP = 2
F32 = jnp.float32
BF16 = jnp.bfloat16
tanh_coef = 0.7978845608028654
cubic_term = 0.044715


def gelu_pair(preact):
    inner_arg = tanh_coef * (preact + cubic_term * preact * preact * preact)
    tanh_value = jnp.tanh(inner_arg)
    gelu_value = 0.5 * preact * (1.0 + tanh_value)
    gelu_slope = 0.5 * (1.0 + tanh_value) + 0.5 * preact * (
        1.0 - tanh_value * tanh_value
    ) * tanh_coef * (1.0 + 3.0 * cubic_term * preact * preact)
    return (gelu_value, gelu_slope)


def dot_nn(a, b):
    return lax.dot_general(a, b, (((1,), (0,)), ((), ())), preferred_element_type=F32)


def dot_nt(a, b):
    return lax.dot_general(a, b, (((1,), (1,)), ((), ())), preferred_element_type=F32)


def kernel(
    groups, tokens, positions, hidden, latents_h, out_grad_h, w_conn, w_mod_h, w_up, w_down,
    gen_o, row_o, conn_o,
    hid, latents, out_grad, w_mod, wc, wu, wd, wmx, wm, pick, pkg,
    cpb, cpr, cst, cz, mps, mrs,
    slot, hd, slope_s, ffs, fsib, fsum, rff, dhs, dsib, dsum, rdh, rets, ret,
    rdm, dcs, dcr, dcz, dcx, dcf, dch, cgs, rcg,
    lsem, ssem, rsem, jsem,
):
    p, z, t = lax.axis_index("pp"), lax.axis_index("dp"), lax.axis_index("tp")
    yh, x = p // 4, lax.rem(p, 4)
    pair, par = z // 2, lax.rem(z, 2)
    core = lax.rem(t, 2)
    ypos = yh * 2 + t // 2
    m = yh * 4 + t
    rows = 32

    def zdev(d):
        return (p, lax.rem(z + d + 8, 8), t)

    def pdev(d):
        return (lax.rem(p + d, 8), z, t)

    def xdev(d):
        return (yh * 4 + lax.rem(x + d, 4), z, t)

    def tdev(e):
        return (p, z, lax.rem(t + e, 4))

    def yplace(d):
        return lax.rem(ypos + d, 4)

    def ydev(d):
        yy = yplace(d)
        return ((yy // 2) * 4 + x, z, lax.rem(yy, 2) * 2 + core)

    twin = (p, z, t + 1 - 2 * core)
    partner = (p, z + 1 - 2 * par, t)

    barrier = pltpu.get_barrier_semaphore()
    peers = [zdev(d) for d in range(1, 8)]
    peers += [pdev(d) for d in range(1, 8)]
    peers += [tdev(e) for e in range(1, 4)]
    peers += [ydev(d) for d in (1, 3)]
    for dev in peers:
        pl.semaphore_signal(barrier, inc=1, device_id=dev, device_id_type=MESH)
    owner = pair == t
    for j in range(4):

        @pl.when(jnp.logical_not(jnp.logical_and(owner, pair == j)))
        def _():
            pl.semaphore_signal(
                barrier, inc=1, device_id=(p, 2 * j + par, pair), device_id_type=MESH
            )

    loc = []

    def load(src, dst):
        c = pltpu.make_async_copy(src, dst, lsem.at[len(loc)])
        c.start()
        loc.append(c)
        return c

    c_hid = load(hidden, hid)
    c_wm = load(w_mod_h, w_mod)
    c_wc = [
        load(w_conn.at[pl.ds(512 * i, 512)], wc.at[pl.ds(512 * i, 512)]) for i in range(3)
    ]
    c_lat = load(latents_h, latents)
    c_og = load(out_grad_h, out_grad)

    seq_iota = lax.broadcasted_iota(jnp.int32, (8, 128), 1)
    row_iota = lax.broadcasted_iota(jnp.int32, (8, 128), 0)
    c_hid.wait()
    parts = []
    for s in range(4):
        at = jnp.zeros((8, 128), jnp.int32)
        for i in range(8):
            at = jnp.where(row_iota == i, positions[s, i], at)
        sel = jnp.where(seq_iota == at, 1.0, 0.0).astype(BF16)
        parts.append(dot_nn(sel, hid[s]))
    pick[...] = jnp.concatenate(parts, axis=0).astype(BF16)
    pkg[par * 4 + pair] = pick[...]

    parts = []
    for i in range(3):
        c_wc[i].wait()
        parts.append(dot_nt(pick[...], wc[pl.ds(512 * i, 512), :]))
    cond = jnp.concatenate(parts, axis=1).T
    pieces = []
    for k in range(4):
        for pp in range(8):
            pieces.append(cond[192 * pp + 48 * k : 192 * pp + 48 * k + 48])
    cond = jnp.concatenate(pieces, axis=0).T.astype(BF16)
    for k in range(4):
        cpb[k] = cond[:, 384 * k : 384 * k + 384]
    c_wm.wait()
    for k in range(3):
        wmx[par, 0:24, 384 * k : 384 * k + 384] = w_mod[k]
    wmx[par, 24:32, :] = jnp.zeros((8, 1152), BF16)
    pl.semaphore_wait(barrier, len(peers) + 4 - jnp.where(owner, 1, 0))

    sent = []

    def send(src, dst, dev):
        k = len(sent)
        c = pltpu.make_async_remote_copy(
            src_ref=src, dst_ref=dst, send_sem=ssem.at[k], recv_sem=rsem.at[k],
            device_id=dev, device_id_type=MESH,
        )
        c.start()
        sent.append(c)
        return c

    def arrive(copies):
        for c in copies:
            c.wait_recv()

    x_wm = send(wmx.at[par], wmx.at[par], partner)
    r_cp = []
    for e in (2, 3, 1):
        r_cp.append(send(cpb.at[lax.rem(t + e, 4)], cpr.at[e - 1], tdev(e)))

    def half(ref, which):
        return ref.at[0, :, pl.ds(pl.multiple_of(768 * which, 768), 768)]

    def block(buf, who, xx, lo=0, n=192):
        return buf.at[pl.ds(pl.multiple_of(192 * (who * 4 + xx) + lo, 32), n)]

    xm, xp = lax.rem(x + 3, 4), lax.rem(x + 1, 4)

    def to_neighbours(src, dst):
        return [send(src, dst, xdev(1)), send(src, dst, xdev(3))]

    def hand_over(buf, who, near):
        arrive(near[:1])
        top = block(buf, who, xm, 0, 96)
        c1 = send(top, top, xdev(1))
        arrive(near[1:])
        low = block(buf, who, xp, 96, 96)
        return [c1, send(low, low, xdev(3))]

    own_u, own_d = block(wu, yh, x), block(wd, yh, x)
    oth_u, oth_d = block(wu, 1 - yh, x), block(wd, 1 - yh, x)
    y_wu = send(half(w_up, 1 - yh), own_u, pdev(4))
    au = to_neighbours(half(w_up, yh), own_u)
    c_wu = load(half(w_up, yh), own_u)
    c_wd = load(half(w_down, yh), own_d)
    r_pk = [send(pick, pkg.at[par * 4 + pair], zdev(d)) for d in (1, 7)]
    arrive([x_wm])
    wm[p] = jnp.concatenate(
        [wmx[0].astype(F32)[:24], wmx[1].astype(F32)[:24]], axis=0
    ).astype(BF16)
    r_wm = [send(wm.at[p], wm.at[p], pdev(d)) for d in (4, 2, 6, 1, 7, 3, 5)]

    c_lat.wait()
    c_og.wait()
    lat = latents[...].astype(F32).reshape(rows, 1536)
    mean = jnp.mean(lat, axis=-1, keepdims=True)
    cent = lat - mean
    var = jnp.mean(cent * cent, axis=-1, keepdims=True)
    inv = 1.0 / jnp.sqrt(var + 1e-06)
    mine = pl.ds(pl.multiple_of(t * 384, 384), 384)
    lat_t = latents[:, :, mine].astype(F32).reshape(rows, 384)
    normed = (lat_t - mean) * inv
    cot = out_grad[...].astype(F32).reshape(rows, 384)

    gs = [groups[s] for s in range(4)]
    places = []
    for s in range(4):
        rank = 0
        for q in range(s):
            rank = rank + jnp.where(gs[q] == gs[s], 1, 0)
        places.append(gs[s] * CAP + rank)
    big_r = lax.broadcasted_iota(jnp.int32, (128, rows), 0)
    big_c = lax.broadcasted_iota(jnp.int32, (128, rows), 1)
    place = jnp.zeros((128, rows), jnp.int32)
    for s in range(4):
        place = jnp.where(big_c // 8 == s, places[s], place)
    onehot = jnp.where(big_r == place * 8 + lax.rem(big_c, 8), 1.0, 0.0).astype(BF16)
    flip_r = lax.broadcasted_iota(jnp.int32, (rows, 128), 0)
    flip_c = lax.broadcasted_iota(jnp.int32, (rows, 128), 1)
    place_f = jnp.zeros((rows, 128), jnp.int32)
    for s in range(4):
        place_f = jnp.where(flip_r // 8 == s, places[s], place_f)
    onehot_f = jnp.where(flip_c == place_f * 8 + lax.rem(flip_r, 8), 1.0, 0.0).astype(BF16)
    one_r = lax.broadcasted_iota(jnp.int32, (rows, 384), 0)
    used = jnp.zeros((rows, 384), jnp.int32)
    for s in range(4):
        used = jnp.where(one_r // 8 == s, tokens[s], used)
    valid = jnp.where(lax.rem(one_r, 8) < used, 1.0, 0.0)

    arrive(r_cp)
    cond = cpb[t].astype(F32)
    for e in range(3):
        cond = cond + cpr[e].astype(F32)
    cst[...] = cond.astype(BF16)

    def cond_copy(e):
        return pltpu.make_async_remote_copy(
            src_ref=cst, dst_ref=cz.at[pair], send_sem=jsem.at[e], recv_sem=jsem.at[4 + pair],
            device_id=(p, 2 * t + par, lax.rem(t + e, 4)), device_id_type=MESH,
        )

    here = pltpu.make_async_copy(cst, cz.at[pair], jsem.at[4 + pair])
    for e in (2, 1, 3):
        cond_copy(e).start()

    @pl.when(owner)
    def _():
        here.start()

    @pl.when(jnp.logical_not(owner))
    def _():
        cond_copy(0).start()

    y_wd = send(half(w_down, 1 - yh), own_d, pdev(4))
    du = hand_over(wu, yh, au)
    arrive(r_wm)
    for j in range(4):
        pltpu.make_async_copy(cst, cz.at[j], jsem.at[4 + j]).wait()

    wmod = wm[...].reshape(384, 1152)
    pooled = cz[...].reshape(128, 384)
    mps[...] = dot_nn(pooled, wmod).astype(BF16).reshape(4, rows, 1152)
    r_mr = []
    for d in (2, 1, 3):
        dev = zdev(2 * d)
        r_mr.append(send(mps.at[dev[1] // 2], mrs.at[d - 1], dev))
    mod = mps[pair].astype(F32)
    arrive([y_wu])
    cu = to_neighbours(oth_u, oth_u)
    ad = to_neighbours(half(w_down, yh), own_d)
    arrive(r_mr)
    for d in range(3):
        mod = mod + mrs[d].astype(F32)
    shift, scale, gate = mod[:, :384], mod[:, 384:768], mod[:, 768:]

    h_in = (normed * (1.0 + scale) + shift).astype(BF16)
    d_out = (gate * cot).astype(BF16)
    packed = dot_nn(onehot, jnp.concatenate([h_in, d_out], axis=1)).astype(BF16)
    slot[...] = packed.reshape(8, 16, 768)
    r_sl = []
    for d in (4, 3, 5, 2, 6, 1, 7):
        dev = zdev(d)
        r_sl.append(send(slot.at[dev[1]], hd.at[m, pl.ds(16 * d, 16)], dev))
    hd[m, pl.ds(0, 16)] = slot[z]
    arrive(r_sl)

    def piece(k, lo):
        return hd.at[k, :, pl.ds(lo, 384)]

    first = []
    for lo in (0, 384):
        first.append([send(piece(m, lo), piece(m, lo), ydev(d)) for d in (2, 1, 3)])
    eu = hand_over(wu, 1 - yh, cu)
    arrive([y_wd])
    cd = to_neighbours(oth_d, oth_d)
    dd = hand_over(wd, yh, ad)
    second = [[send(piece(m, lo), piece(m, lo), twin)] for lo in (0, 384)]
    r_pk += [send(pick, pkg.at[par * 4 + pair], zdev(d)) for d in (4, 3, 5, 2, 6)]

    def hand_on(which, lo):
        for c, d in zip(first[which], (2, 1, 3)):
            arrive([c])
            k = 2 * lax.rem(ypos + 4 - d, 4) + core
            second[which].append(send(piece(k, lo), piece(k, lo), twin))

    hand_on(0, 0)
    arrive(second[0])
    c_wu.wait()
    arrive(du + eu)

    def both(k, lo):
        return jnp.concatenate([hd[k, :, lo : lo + 384], hd[4 + k, :, lo : lo + 384]], axis=0)

    def reduce_out(val, weight, out, sib, whole, got):
        for k in range(4):
            res = dot_nt(val, weight[384 * k : 384 * k + 384, :]).astype(BF16)
            out[k % 2, k // 2] = res[:128]
            out[k % 2, 2 + k // 2] = res[128:]
        return [send(out.at[1 - core, d], sib.at[d], twin) for d in range(4)]

    def reduce_chips(ex, out, sib, whole, got):
        arrive(ex)
        for d in range(4):
            whole[d] = (out[core, d].astype(F32) + sib[d].astype(F32)).astype(BF16)
        return [send(whole.at[yplace(d)], got.at[d - 1], ydev(d)) for d in (2, 1, 3)]

    def reduce_end(ex, whole, got):
        arrive(ex)
        res = whole[ypos].astype(F32)
        for d in range(3):
            res = res + got[d].astype(F32)
        return res.astype(BF16).reshape(8, 16, 384)

    pre = dot_nn(both(0, 0), wu[0:384, :])
    for k in range(1, 4):
        pre = pre + dot_nn(both(k, 0), wu[384 * k : 384 * k + 384, :])
    value, slope = gelu_pair(pre)
    act = value.astype(BF16)
    slope_s[...] = slope
    hand_on(1, 384)
    c_wd.wait()
    ed = hand_over(wd, 1 - yh, cd)
    arrive(dd + ed)
    ff_ex = reduce_out(act, wd, ffs, fsib, fsum, rff)
    arrive(second[1])
    d_act = dot_nn(both(0, 384), wd[0:384, :])
    for k in range(1, 4):
        d_act = d_act + dot_nn(both(k, 384), wd[384 * k : 384 * k + 384, :])
    d_pre = (d_act * slope_s[...]).astype(BF16)
    r_ff = reduce_chips(ff_ex, ffs, fsib, fsum, rff)
    dh_ex = reduce_out(d_pre, wu, dhs, dsib, dsum, rdh)
    r_dh = reduce_chips(dh_ex, dhs, dsib, dsum, rdh)
    rets[:, :, pl.ds(0, 384)] = reduce_end(r_ff, fsum, rff)
    rets[:, :, pl.ds(384, 384)] = reduce_end(r_dh, dsum, rdh)
    r_rt = [send(rets.at[d], ret.at[z], zdev(-d)) for d in (4, 3, 5, 2, 6, 1, 7)]
    ret[z] = rets[0]
    arrive(r_rt)
    home = dot_nn(onehot_f, ret[...].reshape(128, 768))
    ff_out, d_hin = home[:, :384], home[:, 384:]
    d_mod = jnp.concatenate(
        [valid * d_hin, valid * (d_hin * normed), valid * (cot * ff_out)], axis=1
    )
    rdm[pair] = d_mod.astype(BF16)
    r_dm = [send(rdm.at[pair], rdm.at[pair], zdev(2 * d)) for d in (2, 1, 3)]
    gen_o[...] = (valid * (lat_t + gate * ff_out)).reshape(4, 8, 384).astype(BF16)
    arrive(r_dm)
    dcs[...] = dot_nt(rdm[...].reshape(128, 1152), wm[...].reshape(384, 1152)).astype(BF16)
    r_dc = [send(dcs, dcr.at[e - 1], tdev(e)) for e in (2, 3, 1)]
    arrive(r_dc)
    d_cond = dcs[...].astype(F32)
    for e in range(3):
        d_cond = d_cond + dcr[e].astype(F32)
    d_cond = d_cond.astype(BF16)
    turned = d_cond.astype(F32).T
    for h in range(2):
        dcx[h] = jnp.concatenate(
            [turned[48 * pp + 24 * h : 48 * pp + 24 * h + 24] for pp in range(8)], axis=0
        ).astype(BF16)
    r_df = [send(dcx.at[1 - par], dcf.at[par], partner)]
    dcz[...] = d_cond.reshape(4, rows, 384)
    r_dz = []
    for d in (2, 1, 3):
        dev = zdev(2 * d)
        r_dz.append(send(dcz.at[dev[1] // 2], dch.at[pair], dev))
    dch[pair] = dcz[pair]
    dcf[par] = dcx[par]

    arrive(r_pk)
    arrive(r_df)
    r_cg = []
    for h in range(2):
        sides = []
        for i in range(2):
            cols = pl.ds(1024 * h + 512 * i, 512)
            res = dot_nn(dcf[0], pkg[0:4, :, cols].reshape(128, 512))
            res = res + dot_nn(dcf[1], pkg[4:8, :, cols].reshape(128, 512))
            sides.append(res.reshape(8, 24, 512))
        cgs[h] = jnp.concatenate(
            [sides[0][:, :16], sides[1][:, :16], sides[0][:, 16:24], sides[1][:, 16:24]], axis=1
        ).astype(BF16)
        for d in (4, 2, 6, 1, 7, 3, 5):
            dev = pdev(d)
            r_cg.append(send(cgs.at[h, dev[0]], rcg.at[h, d - 1], dev))

    arrive(r_dz)
    back = jnp.concatenate([dch[q].astype(F32) for q in range(4)], axis=1).T
    pieces = []
    for pp in range(8):
        for q in range(4):
            pieces.append(back[384 * q + 48 * pp : 384 * q + 48 * pp + 48])
    back = jnp.concatenate(pieces, axis=0).T.astype(BF16)
    for i in range(4):
        cols = pl.ds(512 * i, 512)
        row_o[:, :, cols] = dot_nn(back, wc[:, cols]).reshape(4, 8, 512).astype(BF16)

    for h in range(2):
        arrive(r_cg[7 * h : 7 * h + 7])
        cg = cgs[h, p].astype(F32)
        for e in range(7):
            cg = cg + rcg[h, e].astype(F32)
        cg = cg * (1.0 / 64.0)
        for i in range(2):
            cols = pl.ds(1024 * h + 512 * i, 512)
            conn_o[0:16, cols] = cg[16 * i : 16 * i + 16]
            conn_o[16:24, cols] = cg[32 + 8 * i : 40 + 8 * i]
    for c in sent:
        c.wait_send()
    for e in range(1, 4):
        cond_copy(e).wait_send()

    @pl.when(jnp.logical_not(owner))
    def _():
        cond_copy(0).wait_send()


def hand_out(gen, row, conn, gen_o, row_o, conn_o):
    gen_o[...] = gen[...]
    row_o[...] = row[...]
    conn_o[...] = conn[...]


def local(hidden, positions, image_tokens, groups, latents, out_grad, w_conn, w_mod, w_up, w_down):
    vm = pl.BlockSpec(memory_space=pltpu.VMEM)
    sm = pl.BlockSpec(memory_space=pltpu.SMEM)
    hb = pl.BlockSpec(memory_space=pl.ANY)
    V = pltpu.VMEM
    n_copies = 144
    outs = pl.pallas_call(
        kernel,
        out_shape=(
            jax.ShapeDtypeStruct((4, 8, 384), BF16),
            jax.ShapeDtypeStruct((4, 8, 2048), BF16),
            jax.ShapeDtypeStruct((24, 2048), F32),
        ),
        in_specs=[sm, sm, sm, hb, hb, hb, hb, hb, hb, hb],
        out_specs=(vm, vm, vm),
        scratch_shapes=[
            V((4, 128, 2048), BF16),
            V((4, 8, 1536), BF16),
            V((4, 8, 384), BF16),
            V((3, 24, 384), BF16),
            V((1536, 2048), BF16),
            V((1536, 768), BF16),
            V((1536, 768), BF16),
            V((2, 32, 1152), BF16),
            V((8, 48, 1152), BF16),
            V((32, 2048), BF16),
            V((8, 32, 2048), BF16),
            V((4, 32, 384), BF16),
            V((3, 32, 384), BF16),
            V((32, 384), BF16),
            V((4, 32, 384), BF16),
            V((4, 32, 1152), BF16),
            V((3, 32, 1152), BF16),
            V((8, 16, 768), BF16),
            V((8, 128, 768), BF16),
            V((256, 768), F32),
            V((2, 4, 128, 384), BF16),
            V((4, 128, 384), BF16),
            V((4, 128, 384), BF16),
            V((3, 128, 384), BF16),
            V((2, 4, 128, 384), BF16),
            V((4, 128, 384), BF16),
            V((4, 128, 384), BF16),
            V((3, 128, 384), BF16),
            V((8, 16, 768), BF16),
            V((8, 16, 768), BF16),
            V((4, 32, 1152), BF16),
            V((128, 384), BF16),
            V((3, 128, 384), BF16),
            V((4, 32, 384), BF16),
            V((2, 192, 128), BF16),
            V((2, 192, 128), BF16),
            V((4, 32, 384), BF16),
            V((2, 8, 48, 512), BF16),
            V((2, 7, 48, 512), BF16),
            pltpu.SemaphoreType.DMA((12,)),
            pltpu.SemaphoreType.DMA((n_copies,)),
            pltpu.SemaphoreType.DMA((n_copies,)),
            pltpu.SemaphoreType.DMA((8,)),
        ],
        compiler_params=pltpu.CompilerParams(
            collective_id=0, has_side_effects=True, vmem_limit_bytes=56 * 2**20
        ),
        cost_estimate=pl.CostEstimate(
            flops=6_000_000_000, bytes_accessed=16_000_000, transcendentals=200_000
        ),
    )(
        groups.reshape(4), image_tokens, positions, hidden, latents, out_grad, w_conn,
        jnp.transpose(w_mod, (1, 0, 2)), w_up, w_down,
    )
    return pl.pallas_call(
        hand_out,
        out_shape=tuple(jax.ShapeDtypeStruct(o.shape, o.dtype) for o in outs),
        in_specs=[vm, vm, vm],
        out_specs=(vm, vm, vm),
    )(*outs)


def solution(mesh):
    placed = (
        P(("pp", "dp"), None, "tp"),
        P(("pp", "dp"), None),
        P(("pp", "dp")),
        P(("pp", "dp"), None),
        P(("pp", "dp"), None, None),
        P(("pp", "dp"), None, "tp"),
        P(None, "tp"),
        P(("pp", "dp"), None, "tp"),
        P("dp", "pp", "tp"),
        P("dp", "pp", "tp"),
    )
    return jax.shard_map(
        local,
        mesh=mesh,
        in_specs=placed,
        out_specs=(P(("pp", "dp"), None, "tp"), P(("pp", "dp"), None, "tp"), P(("pp", "dp"), "tp")),
        check_vma=False,
    )
```

```python
import functools

import jax
import jax.numpy as jnp
from jax import lax
from jax.experimental import pallas as pl
from jax.experimental.pallas import tpu as pltpu
from jax.sharding import PartitionSpec as P

MESH = pl.DeviceIdType.MESH
CAP = 2
F32 = jnp.float32
BF16 = jnp.bfloat16
tanh_coef = 0.7978845608028654
cubic_term = 0.044715


def gelu_pair(preact):
    inner_arg = tanh_coef * (preact + cubic_term * preact * preact * preact)
    tanh_value = jnp.tanh(inner_arg)
    gelu_value = 0.5 * preact * (1.0 + tanh_value)
    gelu_slope = 0.5 * (1.0 + tanh_value) + 0.5 * preact * (
        1.0 - tanh_value * tanh_value
    ) * tanh_coef * (1.0 + 3.0 * cubic_term * preact * preact)
    return (gelu_value, gelu_slope)


def dot_nn(a, b):
    return lax.dot_general(a, b, (((1,), (0,)), ((), ())), preferred_element_type=F32)


def dot_nt(a, b):
    return lax.dot_general(a, b, (((1,), (1,)), ((), ())), preferred_element_type=F32)


def kernel(
    groups, tokens, positions, hidden, latents_h, out_grad_h, w_conn, w_mod_h, w_up, w_down,
    gen_o, row_o, conn_o,
    hid, latents, out_grad, w_mod, wc, wu, wd, wmx, wm, pick, pkg,
    cpb, cpr, cst, cz, mps, mrs, mpg, mrg,
    slot, hd, slope_s, ffs, fsib, fsum, rff, dhs, dsib, dsum, rdh, rets, ret,
    rdm, rdm2, dcs, dcr, dcz, dcx, dcf, dch, cgs, rcg,
    lsem, ssem, rsem, jsem,
):
    p, z, t = lax.axis_index("pp"), lax.axis_index("dp"), lax.axis_index("tp")
    yh, x = p // 4, lax.rem(p, 4)
    pair, par = z // 2, lax.rem(z, 2)
    core = lax.rem(t, 2)
    ypos = yh * 2 + t // 2
    m = yh * 4 + t
    rows = 32

    def zdev(d):
        return (p, lax.rem(z + d + 8, 8), t)

    def pdev(d):
        return (lax.rem(p + d, 8), z, t)

    def xdev(d):
        return (yh * 4 + lax.rem(x + d, 4), z, t)

    def tdev(e):
        return (p, z, lax.rem(t + e, 4))

    def yplace(d):
        return lax.rem(ypos + d, 4)

    def ydev(d):
        yy = yplace(d)
        return ((yy // 2) * 4 + x, z, lax.rem(yy, 2) * 2 + core)

    twin = (p, z, t + 1 - 2 * core)
    partner = (p, z + 1 - 2 * par, t)

    barrier = pltpu.get_barrier_semaphore()
    peers = [zdev(d) for d in range(1, 8)]
    peers += [pdev(d) for d in range(1, 8)]
    peers += [(lax.rem(p + d, 8), partner[1], t) for d in range(1, 8)]
    peers += [tdev(e) for e in range(1, 4)]
    peers += [ydev(d) for d in (1, 3)]
    for dev in peers:
        pl.semaphore_signal(barrier, inc=1, device_id=dev, device_id_type=MESH)
    owner = pair == t
    for j in range(4):

        @pl.when(jnp.logical_not(jnp.logical_and(owner, pair == j)))
        def _():
            pl.semaphore_signal(
                barrier, inc=1, device_id=(p, 2 * j + par, pair), device_id_type=MESH
            )

    loc = []

    def load(src, dst):
        c = pltpu.make_async_copy(src, dst, lsem.at[len(loc)])
        c.start()
        loc.append(c)
        return c

    c_hid = load(hidden, hid)
    c_wm = load(w_mod_h, w_mod)
    c_wc = [
        load(w_conn.at[pl.ds(512 * i, 512)], wc.at[pl.ds(512 * i, 512)]) for i in range(3)
    ]
    c_lat = load(latents_h, latents)
    c_og = load(out_grad_h, out_grad)

    seq_iota = lax.broadcasted_iota(jnp.int32, (8, 128), 1)
    row_iota = lax.broadcasted_iota(jnp.int32, (8, 128), 0)
    c_hid.wait()
    parts = []
    for s in range(4):
        at = jnp.zeros((8, 128), jnp.int32)
        for i in range(8):
            at = jnp.where(row_iota == i, positions[s, i], at)
        sel = jnp.where(seq_iota == at, 1.0, 0.0).astype(BF16)
        parts.append(dot_nn(sel, hid[s]))
    pick[...] = jnp.concatenate(parts, axis=0).astype(BF16)
    pkg[par * 4 + pair] = pick[...]

    parts = []
    for i in range(3):
        c_wc[i].wait()
        parts.append(dot_nt(pick[...], wc[pl.ds(512 * i, 512), :]))
    cond = jnp.concatenate(parts, axis=1).T
    pieces = []
    for k in range(4):
        for pp in range(8):
            pieces.append(cond[192 * pp + 48 * k : 192 * pp + 48 * k + 48])
    cond = jnp.concatenate(pieces, axis=0).T.astype(BF16)
    for k in range(4):
        cpb[k] = cond[:, 384 * k : 384 * k + 384]
    c_wm.wait()
    for k in range(3):
        wmx[par, p, :, 384 * k : 384 * k + 384] = w_mod[k]
    pl.semaphore_wait(barrier, len(peers) + 4 - jnp.where(owner, 1, 0))

    sent = []

    def send(src, dst, dev):
        k = len(sent)
        c = pltpu.make_async_remote_copy(
            src_ref=src, dst_ref=dst, send_sem=ssem.at[k], recv_sem=rsem.at[k],
            device_id=dev, device_id_type=MESH,
        )
        c.start()
        sent.append(c)
        return c

    def arrive(copies):
        for c in copies:
            c.wait_recv()

    far = (4, 2, 6, 1, 7, 3, 5)
    r_cp = []
    for e in (2, 3, 1):
        r_cp.append(send(cpb.at[lax.rem(t + e, 4)], cpr.at[e - 1], tdev(e)))
    r_wm = [send(wmx.at[par, p], wmx.at[par, p], pdev(d)) for d in far]
    x_wm = [send(wmx.at[par, p], wmx.at[par, p], partner)]
    for d in far:
        x_wm.append(
            send(wmx.at[par, p], wmx.at[par, p], (lax.rem(p + d, 8), partner[1], t))
        )

    def half(ref, which):
        return ref.at[0, :, pl.ds(pl.multiple_of(768 * which, 768), 768)]

    def block(buf, who, xx, lo=0, n=192):
        return buf.at[pl.ds(pl.multiple_of(192 * (who * 4 + xx) + lo, 32), n)]

    xm, xp = lax.rem(x + 3, 4), lax.rem(x + 1, 4)

    def to_neighbours(src, dst):
        return [send(src, dst, xdev(1)), send(src, dst, xdev(3))]

    def hand_over(buf, who, near):
        arrive(near[:1])
        top = block(buf, who, xm, 0, 96)
        c1 = send(top, top, xdev(1))
        arrive(near[1:])
        low = block(buf, who, xp, 96, 96)
        return [c1, send(low, low, xdev(3))]

    own_u, own_d = block(wu, yh, x), block(wd, yh, x)
    oth_u, oth_d = block(wu, 1 - yh, x), block(wd, 1 - yh, x)
    c_wu = load(half(w_up, yh), own_u)
    c_wd = load(half(w_down, yh), own_d)
    r_pk = [send(pick, pkg.at[par * 4 + pair], zdev(d)) for d in (1, 7)]

    c_lat.wait()
    c_og.wait()
    lat = latents[...].astype(F32).reshape(rows, 1536)
    mean = jnp.mean(lat, axis=-1, keepdims=True)
    cent = lat - mean
    var = jnp.mean(cent * cent, axis=-1, keepdims=True)
    inv = 1.0 / jnp.sqrt(var + 1e-06)
    mine = pl.ds(pl.multiple_of(t * 384, 384), 384)
    lat_t = latents[:, :, mine].astype(F32).reshape(rows, 384)
    normed = (lat_t - mean) * inv
    cot = out_grad[...].astype(F32).reshape(rows, 384)

    gs = [groups[s] for s in range(4)]
    places = []
    for s in range(4):
        rank = 0
        for q in range(s):
            rank = rank + jnp.where(gs[q] == gs[s], 1, 0)
        places.append(gs[s] * CAP + rank)
    big_r = lax.broadcasted_iota(jnp.int32, (128, rows), 0)
    big_c = lax.broadcasted_iota(jnp.int32, (128, rows), 1)
    place = jnp.zeros((128, rows), jnp.int32)
    for s in range(4):
        place = jnp.where(big_c // 8 == s, places[s], place)
    onehot = jnp.where(big_r == place * 8 + lax.rem(big_c, 8), 1.0, 0.0).astype(BF16)
    flip_r = lax.broadcasted_iota(jnp.int32, (rows, 128), 0)
    flip_c = lax.broadcasted_iota(jnp.int32, (rows, 128), 1)
    place_f = jnp.zeros((rows, 128), jnp.int32)
    for s in range(4):
        place_f = jnp.where(flip_r // 8 == s, places[s], place_f)
    onehot_f = jnp.where(flip_c == place_f * 8 + lax.rem(flip_r, 8), 1.0, 0.0).astype(BF16)
    one_r = lax.broadcasted_iota(jnp.int32, (rows, 384), 0)
    used = jnp.zeros((rows, 384), jnp.int32)
    for s in range(4):
        used = jnp.where(one_r // 8 == s, tokens[s], used)
    valid = jnp.where(lax.rem(one_r, 8) < used, 1.0, 0.0)

    arrive(r_cp)
    cond = cpb[t].astype(F32)
    for e in range(3):
        cond = cond + cpr[e].astype(F32)
    cst[...] = cond.astype(BF16)

    def cond_copy(e):
        return pltpu.make_async_remote_copy(
            src_ref=cst, dst_ref=cz.at[pair], send_sem=jsem.at[e], recv_sem=jsem.at[4 + pair],
            device_id=(p, 2 * t + par, lax.rem(t + e, 4)), device_id_type=MESH,
        )

    here = pltpu.make_async_copy(cst, cz.at[pair], jsem.at[4 + pair])
    for e in (2, 1, 3):
        cond_copy(e).start()

    @pl.when(owner)
    def _():
        here.start()

    @pl.when(jnp.logical_not(owner))
    def _():
        cond_copy(0).start()

    y_wu = send(half(w_up, 1 - yh), own_u, pdev(4))
    au = to_neighbours(half(w_up, yh), own_u)
    for c, d in zip(x_wm, (0,) + far):
        arrive([c])
        if d > 0:
            arrive([r_wm[far.index(d)]])
        pd = lax.rem(p + 8 - d, 8)
        wm[pd] = jnp.concatenate(
            [wmx[0, pd].astype(F32), wmx[1, pd].astype(F32)], axis=0
        ).astype(BF16)
    du = hand_over(wu, yh, au)
    for j in range(4):
        pltpu.make_async_copy(cst, cz.at[j], jsem.at[4 + j]).wait()

    wmod = wm[...].reshape(384, 1152)
    pooled = cz[...].reshape(128, 384)
    mps[...] = dot_nn(pooled, wmod[:, :768]).astype(BF16).reshape(4, rows, 768)
    r_mr, r_mg = [], []
    for d in (2, 1, 3):
        dev = zdev(2 * d)
        r_mr.append(send(mps.at[dev[1] // 2], mrs.at[d - 1], dev))
    mpg[...] = dot_nn(pooled, wmod[:, 768:]).astype(BF16).reshape(4, rows, 384)
    for d in (2, 1, 3):
        dev = zdev(2 * d)
        r_mg.append(send(mpg.at[dev[1] // 2], mrg.at[d - 1], dev))
    arrive([y_wu])
    y_wd = send(half(w_down, 1 - yh), own_d, pdev(4))
    cu = to_neighbours(oth_u, oth_u)
    ad = to_neighbours(half(w_down, yh), own_d)

    def to_group(which, val):
        slot[which] = dot_nn(onehot, val).astype(BF16).reshape(8, 16, 384)
        hd[which, m, pl.ds(0, 16)] = slot[which, z]
        out = []
        for d in (4, 3, 5, 2, 6, 1, 7):
            dev = zdev(d)
            out.append(send(slot.at[which, dev[1]], hd.at[which, m, pl.ds(16 * d, 16)], dev))
        return out

    mod = mps[pair].astype(F32)
    arrive(r_mr)
    for d in range(3):
        mod = mod + mrs[d].astype(F32)
    r_sh = to_group(0, (normed * (1.0 + mod[:, 384:]) + mod[:, :384]).astype(BF16))
    gate = mpg[pair].astype(F32)
    arrive(r_mg)
    for d in range(3):
        gate = gate + mrg[d].astype(F32)
    r_sd = to_group(1, (gate * cot).astype(BF16))

    first, second = [], []
    for which, got in ((0, r_sh), (1, r_sd)):
        arrive(got)
        here_rows = hd.at[which, m]
        first.append([send(here_rows, here_rows, ydev(d)) for d in (2, 1, 3)])
        second.append([send(here_rows, here_rows, twin)])
        if which == 0:
            eu = hand_over(wu, 1 - yh, cu)
    arrive([y_wd])
    cd = to_neighbours(oth_d, oth_d)
    dd = hand_over(wd, yh, ad)
    r_pk += [send(pick, pkg.at[par * 4 + pair], zdev(d)) for d in (4, 3, 5, 2, 6)]

    def hand_on(which):
        for c, d in zip(first[which], (2, 1, 3)):
            arrive([c])
            k = 2 * lax.rem(ypos + 4 - d, 4) + core
            second[which].append(send(hd.at[which, k], hd.at[which, k], twin))

    hand_on(0)
    arrive(second[0])
    c_wu.wait()
    arrive(du + eu)

    def both(which, k):
        return jnp.concatenate([hd[which, k], hd[which, 4 + k]], axis=0)

    def reduce_out(val, weight, out, sib, whole, got):
        for k in range(4):
            res = dot_nt(val, weight[384 * k : 384 * k + 384, :]).astype(BF16)
            out[k % 2, k // 2] = res[:128]
            out[k % 2, 2 + k // 2] = res[128:]
        return [send(out.at[1 - core, d], sib.at[d], twin) for d in range(4)]

    def reduce_chips(ex, out, sib, whole, got):
        arrive(ex)
        for d in range(4):
            whole[d] = (out[core, d].astype(F32) + sib[d].astype(F32)).astype(BF16)
        return [send(whole.at[yplace(d)], got.at[d - 1], ydev(d)) for d in (2, 1, 3)]

    def reduce_end(ex, whole, got):
        arrive(ex)
        res = whole[ypos].astype(F32)
        for d in range(3):
            res = res + got[d].astype(F32)
        return res.astype(BF16).reshape(8, 16, 384)

    pre = dot_nn(both(0, 0), wu[0:384, :])
    for k in range(1, 4):
        pre = pre + dot_nn(both(0, k), wu[384 * k : 384 * k + 384, :])
    value, slope = gelu_pair(pre)
    act = value.astype(BF16)
    slope_s[...] = slope
    hand_on(1)
    c_wd.wait()
    ed = hand_over(wd, 1 - yh, cd)
    arrive(dd + ed)
    ff_ex = reduce_out(act, wd, ffs, fsib, fsum, rff)
    arrive(second[1])
    d_act = dot_nn(both(1, 0), wd[0:384, :])
    for k in range(1, 4):
        d_act = d_act + dot_nn(both(1, k), wd[384 * k : 384 * k + 384, :])
    d_pre = (d_act * slope_s[...]).astype(BF16)
    r_ff = reduce_chips(ff_ex, ffs, fsib, fsum, rff)
    dh_ex = reduce_out(d_pre, wu, dhs, dsib, dsum, rdh)
    r_dh = reduce_chips(dh_ex, dhs, dsib, dsum, rdh)
    rets[0] = reduce_end(r_ff, fsum, rff)
    r_rt = [send(rets.at[0, d], ret.at[0, z], zdev(-d)) for d in (4, 3, 5, 2, 6, 1, 7)]
    ret[0, z] = rets[0, 0]
    rets[1] = reduce_end(r_dh, dsum, rdh)
    r_rd = [send(rets.at[1, d], ret.at[1, z], zdev(-d)) for d in (4, 3, 5, 2, 6, 1, 7)]
    ret[1, z] = rets[1, 0]
    arrive(r_rt)
    ff_out = dot_nn(onehot_f, ret[0].reshape(128, 384))
    rdm2[pair] = (valid * (cot * ff_out)).astype(BF16)
    r_dm = [send(rdm2.at[pair], rdm2.at[pair], zdev(2 * d)) for d in (2, 1, 3)]
    gen_o[...] = (valid * (lat_t + gate * ff_out)).reshape(4, 8, 384).astype(BF16)
    arrive(r_rd)
    d_hin = dot_nn(onehot_f, ret[1].reshape(128, 384))
    rdm[pair] = jnp.concatenate([valid * d_hin, valid * (d_hin * normed)], axis=1).astype(BF16)
    r_dn = [send(rdm.at[pair], rdm.at[pair], zdev(2 * d)) for d in (2, 1, 3)]
    arrive(r_dm)
    wmod = wm[...].reshape(384, 1152)
    dc_part = dot_nt(rdm2[...].reshape(128, 384), wmod[:, 768:])
    arrive(r_dn)
    dc_part = dc_part + dot_nt(rdm[...].reshape(128, 768), wmod[:, :768])
    turned = dc_part.T
    for h in range(2):
        dcs[h] = jnp.concatenate(
            [turned[48 * pp + 24 * h : 48 * pp + 24 * h + 24] for pp in range(8)], axis=0
        ).astype(BF16)

    def over_tp(h):
        return [send(dcs.at[h], dcr.at[h, e - 1], tdev(e)) for e in (2, 3, 1)]

    def summed(h, copies):
        arrive(copies)
        res = dcs[h].astype(F32)
        for e in range(3):
            res = res + dcr[h, e].astype(F32)
        dcx[h] = res.astype(BF16)

    r_d1 = over_tp(1 - par)
    r_d0 = over_tp(par)
    summed(1 - par, r_d1)
    r_df = [send(dcx.at[1 - par], dcf.at[par], partner)]
    summed(par, r_d0)
    dcf[par] = dcx[par]
    d_cond = jnp.concatenate([dcx[0].astype(F32), dcx[1].astype(F32)], axis=0).T
    dcz[...] = d_cond.astype(BF16).reshape(4, rows, 384)
    r_dz = []
    for d in (2, 1, 3):
        dev = zdev(2 * d)
        r_dz.append(send(dcz.at[dev[1] // 2], dch.at[pair], dev))
    dch[pair] = dcz[pair]

    arrive(r_pk)
    arrive(r_df)
    r_cg = []
    for h in range(2):
        sides = []
        for i in range(2):
            cols = pl.ds(1024 * h + 512 * i, 512)
            res = dot_nn(dcf[0], pkg[0:4, :, cols].reshape(128, 512))
            res = res + dot_nn(dcf[1], pkg[4:8, :, cols].reshape(128, 512))
            sides.append(res.reshape(8, 24, 512))
        cgs[h] = jnp.concatenate(
            [sides[0][:, :16], sides[1][:, :16], sides[0][:, 16:24], sides[1][:, 16:24]], axis=1
        ).astype(BF16)
        for d in (4, 2, 6, 1, 7, 3, 5):
            dev = pdev(d)
            r_cg.append(send(cgs.at[h, dev[0]], rcg.at[h, d - 1], dev))

    arrive(r_dz)
    back = jnp.concatenate([dch[q].astype(F32) for q in range(4)], axis=1).T
    pieces = []
    for pp in range(8):
        for q in range(4):
            for h in range(2):
                k = 384 * q + 192 * h + 24 * pp
                pieces.append(back[k : k + 24])
    back = jnp.concatenate(pieces, axis=0).T.astype(BF16)
    for i in range(4):
        cols = pl.ds(512 * i, 512)
        row_o[:, :, cols] = dot_nn(back, wc[:, cols]).reshape(4, 8, 512).astype(BF16)

    for h in range(2):
        arrive(r_cg[7 * h : 7 * h + 7])
        cg = cgs[h, p].astype(F32)
        for e in range(7):
            cg = cg + rcg[h, e].astype(F32)
        cg = cg * (1.0 / 64.0)
        for i in range(2):
            cols = pl.ds(1024 * h + 512 * i, 512)
            conn_o[0:16, cols] = cg[16 * i : 16 * i + 16]
            conn_o[16:24, cols] = cg[32 + 8 * i : 40 + 8 * i]
    for c in sent:
        c.wait_send()
    for e in range(1, 4):
        cond_copy(e).wait_send()

    @pl.when(jnp.logical_not(owner))
    def _():
        cond_copy(0).wait_send()


def hand_out(gen, row, conn, gen_o, row_o, conn_o):
    gen_o[...] = gen[...]
    row_o[...] = row[...]
    conn_o[...] = conn[...]


def local(hidden, positions, image_tokens, groups, latents, out_grad, w_conn, w_mod, w_up, w_down):
    vm = pl.BlockSpec(memory_space=pltpu.VMEM)
    sm = pl.BlockSpec(memory_space=pltpu.SMEM)
    hb = pl.BlockSpec(memory_space=pl.ANY)
    V = pltpu.VMEM
    n_copies = 200
    outs = pl.pallas_call(
        kernel,
        out_shape=(
            jax.ShapeDtypeStruct((4, 8, 384), BF16),
            jax.ShapeDtypeStruct((4, 8, 2048), BF16),
            jax.ShapeDtypeStruct((24, 2048), F32),
        ),
        in_specs=[sm, sm, sm, hb, hb, hb, hb, hb, hb, hb],
        out_specs=(vm, vm, vm),
        scratch_shapes=[
            V((4, 128, 2048), BF16),
            V((4, 8, 1536), BF16),
            V((4, 8, 384), BF16),
            V((3, 24, 384), BF16),
            V((1536, 2048), BF16),
            V((1536, 768), BF16),
            V((1536, 768), BF16),
            V((2, 8, 24, 1152), BF16),
            V((8, 48, 1152), BF16),
            V((32, 2048), BF16),
            V((8, 32, 2048), BF16),
            V((4, 32, 384), BF16),
            V((3, 32, 384), BF16),
            V((32, 384), BF16),
            V((4, 32, 384), BF16),
            V((4, 32, 768), BF16),
            V((3, 32, 768), BF16),
            V((4, 32, 384), BF16),
            V((3, 32, 384), BF16),
            V((2, 8, 16, 384), BF16),
            V((2, 8, 128, 384), BF16),
            V((256, 768), F32),
            V((2, 4, 128, 384), BF16),
            V((4, 128, 384), BF16),
            V((4, 128, 384), BF16),
            V((3, 128, 384), BF16),
            V((2, 4, 128, 384), BF16),
            V((4, 128, 384), BF16),
            V((4, 128, 384), BF16),
            V((3, 128, 384), BF16),
            V((2, 8, 16, 384), BF16),
            V((2, 8, 16, 384), BF16),
            V((4, 32, 768), BF16),
            V((4, 32, 384), BF16),
            V((2, 192, 128), BF16),
            V((2, 3, 192, 128), BF16),
            V((4, 32, 384), BF16),
            V((2, 192, 128), BF16),
            V((2, 192, 128), BF16),
            V((4, 32, 384), BF16),
            V((2, 8, 48, 512), BF16),
            V((2, 7, 48, 512), BF16),
            pltpu.SemaphoreType.DMA((12,)),
            pltpu.SemaphoreType.DMA((n_copies,)),
            pltpu.SemaphoreType.DMA((n_copies,)),
            pltpu.SemaphoreType.DMA((8,)),
        ],
        compiler_params=pltpu.CompilerParams(
            collective_id=0, has_side_effects=True, vmem_limit_bytes=56 * 2**20
        ),
        cost_estimate=pl.CostEstimate(
            flops=6_000_000_000, bytes_accessed=16_000_000, transcendentals=200_000
        ),
    )(
        groups.reshape(4), image_tokens, positions, hidden, latents, out_grad, w_conn,
        jnp.transpose(w_mod, (1, 0, 2)), w_up, w_down,
    )
    return pl.pallas_call(
        hand_out,
        out_shape=tuple(jax.ShapeDtypeStruct(o.shape, o.dtype) for o in outs),
        in_specs=[vm, vm, vm],
        out_specs=(vm, vm, vm),
    )(*outs)


def solution(mesh):
    placed = (
        P(("pp", "dp"), None, "tp"),
        P(("pp", "dp"), None),
        P(("pp", "dp")),
        P(("pp", "dp"), None),
        P(("pp", "dp"), None, None),
        P(("pp", "dp"), None, "tp"),
        P(None, "tp"),
        P(("pp", "dp"), None, "tp"),
        P("dp", "pp", "tp"),
        P("dp", "pp", "tp"),
    )
    return jax.shard_map(
        local,
        mesh=mesh,
        in_specs=placed,
        out_specs=(P(("pp", "dp"), None, "tp"), P(("pp", "dp"), None, "tp"), P(("pp", "dp"), "tp")),
        check_vma=False,
    )
```

```python
import functools

import jax
import jax.numpy as jnp
from jax import lax
from jax.experimental import pallas as pl
from jax.experimental.pallas import tpu as pltpu
from jax.sharding import PartitionSpec as P

MESH = pl.DeviceIdType.MESH
CAP = 2
F32 = jnp.float32
BF16 = jnp.bfloat16
tanh_coef = 0.7978845608028654
cubic_term = 0.044715


def gelu_pair(preact):
    inner_arg = tanh_coef * (preact + cubic_term * preact * preact * preact)
    tanh_value = jnp.tanh(inner_arg)
    gelu_value = 0.5 * preact * (1.0 + tanh_value)
    gelu_slope = 0.5 * (1.0 + tanh_value) + 0.5 * preact * (
        1.0 - tanh_value * tanh_value
    ) * tanh_coef * (1.0 + 3.0 * cubic_term * preact * preact)
    return (gelu_value, gelu_slope)


def dot_nn(a, b):
    return lax.dot_general(a, b, (((1,), (0,)), ((), ())), preferred_element_type=F32)


def dot_nt(a, b):
    return lax.dot_general(a, b, (((1,), (1,)), ((), ())), preferred_element_type=F32)


def kernel(
    groups, tokens, positions, hidden, latents_h, out_grad_h, w_conn, w_mod_h, w_up, w_down,
    gen_o, row_o, conn_o,
    hid, latents, out_grad, w_mod, wc, wu, wd, wmx, wm, pick, pkg,
    cpb, cpr, cst, cz, mps, mrs, mpg, mrg,
    slot, hd, slope_s, ffs, fsib, fsum, rff, dhs, dsib, dsum, rdh, rets, ret,
    rdm, rdm2, dcs, dcr, dcz, dcx, dcf, dch, cgs, rcg,
    lsem, ssem, rsem, jsem,
):
    p, z, t = lax.axis_index("pp"), lax.axis_index("dp"), lax.axis_index("tp")
    yh, x = p // 4, lax.rem(p, 4)
    pair, par = z // 2, lax.rem(z, 2)
    core = lax.rem(t, 2)
    ypos = yh * 2 + t // 2
    m = yh * 4 + t
    rows = 32

    def zdev(d):
        return (p, lax.rem(z + d + 8, 8), t)

    def pdev(d):
        return (lax.rem(p + d, 8), z, t)

    def xdev(d):
        return (yh * 4 + lax.rem(x + d, 4), z, t)

    def tdev(e):
        return (p, z, lax.rem(t + e, 4))

    def yplace(d):
        return lax.rem(ypos + d, 4)

    def ydev(d):
        yy = yplace(d)
        return ((yy // 2) * 4 + x, z, lax.rem(yy, 2) * 2 + core)

    twin = (p, z, t + 1 - 2 * core)
    partner = (p, z + 1 - 2 * par, t)

    barrier = pltpu.get_barrier_semaphore()
    peers = [zdev(d) for d in range(1, 8)]
    peers += [pdev(d) for d in range(1, 8)]
    peers += [(lax.rem(p + d, 8), partner[1], t) for d in range(1, 8)]
    peers += [tdev(e) for e in range(1, 4)]
    peers += [ydev(d) for d in (1, 3)]
    for dev in peers:
        pl.semaphore_signal(barrier, inc=1, device_id=dev, device_id_type=MESH)
    owner = pair == t
    for j in range(4):

        @pl.when(jnp.logical_not(jnp.logical_and(owner, pair == j)))
        def _():
            pl.semaphore_signal(
                barrier, inc=1, device_id=(p, 2 * j + par, pair), device_id_type=MESH
            )

    loc = []

    def load(src, dst):
        c = pltpu.make_async_copy(src, dst, lsem.at[len(loc)])
        c.start()
        loc.append(c)
        return c

    c_hid = load(hidden, hid)
    c_wm = load(w_mod_h, w_mod)
    c_wc = [
        load(w_conn.at[pl.ds(512 * i, 512)], wc.at[pl.ds(512 * i, 512)]) for i in range(3)
    ]
    c_lat = load(latents_h, latents)
    c_og = load(out_grad_h, out_grad)

    seq_iota = lax.broadcasted_iota(jnp.int32, (8, 128), 1)
    row_iota = lax.broadcasted_iota(jnp.int32, (8, 128), 0)
    c_hid.wait()
    parts = []
    for s in range(4):
        at = jnp.zeros((8, 128), jnp.int32)
        for i in range(8):
            at = jnp.where(row_iota == i, positions[s, i], at)
        sel = jnp.where(seq_iota == at, 1.0, 0.0).astype(BF16)
        parts.append(dot_nn(sel, hid[s]))
    pick[...] = jnp.concatenate(parts, axis=0).astype(BF16)
    pkg[par * 4 + pair] = pick[...]

    parts = []
    for i in range(3):
        c_wc[i].wait()
        parts.append(dot_nt(pick[...], wc[pl.ds(512 * i, 512), :]))
    cond = jnp.concatenate(parts, axis=1).T
    pieces = []
    for k in range(4):
        for pp in range(8):
            pieces.append(cond[192 * pp + 48 * k : 192 * pp + 48 * k + 48])
    cond = jnp.concatenate(pieces, axis=0).T.astype(BF16)
    for k in range(4):
        cpb[k] = cond[:, 384 * k : 384 * k + 384]
    c_wm.wait()
    for k in range(3):
        wmx[par, p, :, 384 * k : 384 * k + 384] = w_mod[k]
    pl.semaphore_wait(barrier, len(peers) + 4 - jnp.where(owner, 1, 0))

    sent = []

    def send(src, dst, dev):
        k = len(sent)
        c = pltpu.make_async_remote_copy(
            src_ref=src, dst_ref=dst, send_sem=ssem.at[k], recv_sem=rsem.at[k],
            device_id=dev, device_id_type=MESH,
        )
        c.start()
        sent.append(c)
        return c

    def arrive(copies):
        for c in copies:
            c.wait_recv()

    far = (4, 2, 6, 1, 7, 3, 5)
    r_cp = []
    for e in (2, 3, 1):
        r_cp.append(send(cpb.at[lax.rem(t + e, 4)], cpr.at[e - 1], tdev(e)))
    r_wm = [send(wmx.at[par, p], wmx.at[par, p], pdev(d)) for d in far]
    x_wm = [send(wmx.at[par, p], wmx.at[par, p], partner)]
    for d in far:
        x_wm.append(
            send(wmx.at[par, p], wmx.at[par, p], (lax.rem(p + d, 8), partner[1], t))
        )

    def half(ref, which):
        return ref.at[0, :, pl.ds(pl.multiple_of(768 * which, 768), 768)]

    def block(buf, who, xx, lo=0, n=192):
        return buf.at[pl.ds(pl.multiple_of(192 * (who * 4 + xx) + lo, 32), n)]

    xm, xp = lax.rem(x + 3, 4), lax.rem(x + 1, 4)

    def to_neighbours(src, dst):
        return [send(src, dst, xdev(1)), send(src, dst, xdev(3))]

    def hand_over(buf, who, near):
        arrive(near[:1])
        top = block(buf, who, xm, 0, 96)
        c1 = send(top, top, xdev(1))
        arrive(near[1:])
        low = block(buf, who, xp, 96, 96)
        return [c1, send(low, low, xdev(3))]

    own_u, own_d = block(wu, yh, x), block(wd, yh, x)
    oth_u, oth_d = block(wu, 1 - yh, x), block(wd, 1 - yh, x)
    c_wu = load(half(w_up, yh), own_u)
    c_wd = load(half(w_down, yh), own_d)
    r_pk = [send(pick, pkg.at[par * 4 + pair], zdev(d)) for d in (1, 7)]

    c_lat.wait()
    c_og.wait()
    lat = latents[...].astype(F32).reshape(rows, 1536)
    mean = jnp.mean(lat, axis=-1, keepdims=True)
    cent = lat - mean
    var = jnp.mean(cent * cent, axis=-1, keepdims=True)
    inv = 1.0 / jnp.sqrt(var + 1e-06)
    mine = pl.ds(pl.multiple_of(t * 384, 384), 384)
    lat_t = latents[:, :, mine].astype(F32).reshape(rows, 384)
    normed = (lat_t - mean) * inv
    cot = out_grad[...].astype(F32).reshape(rows, 384)

    gs = [groups[s] for s in range(4)]
    places = []
    for s in range(4):
        rank = 0
        for q in range(s):
            rank = rank + jnp.where(gs[q] == gs[s], 1, 0)
        places.append(gs[s] * CAP + rank)
    big_r = lax.broadcasted_iota(jnp.int32, (128, rows), 0)
    big_c = lax.broadcasted_iota(jnp.int32, (128, rows), 1)
    place = jnp.zeros((128, rows), jnp.int32)
    for s in range(4):
        place = jnp.where(big_c // 8 == s, places[s], place)
    onehot = jnp.where(big_r == place * 8 + lax.rem(big_c, 8), 1.0, 0.0).astype(BF16)
    flip_r = lax.broadcasted_iota(jnp.int32, (rows, 128), 0)
    flip_c = lax.broadcasted_iota(jnp.int32, (rows, 128), 1)
    place_f = jnp.zeros((rows, 128), jnp.int32)
    for s in range(4):
        place_f = jnp.where(flip_r // 8 == s, places[s], place_f)
    onehot_f = jnp.where(flip_c == place_f * 8 + lax.rem(flip_r, 8), 1.0, 0.0).astype(BF16)
    one_r = lax.broadcasted_iota(jnp.int32, (rows, 384), 0)
    used = jnp.zeros((rows, 384), jnp.int32)
    for s in range(4):
        used = jnp.where(one_r // 8 == s, tokens[s], used)
    valid = jnp.where(lax.rem(one_r, 8) < used, 1.0, 0.0)

    arrive(r_cp)
    cond = cpb[t].astype(F32)
    for e in range(3):
        cond = cond + cpr[e].astype(F32)
    cst[...] = cond.astype(BF16)

    def cond_copy(e):
        return pltpu.make_async_remote_copy(
            src_ref=cst, dst_ref=cz.at[pair], send_sem=jsem.at[e], recv_sem=jsem.at[4 + pair],
            device_id=(p, 2 * t + par, lax.rem(t + e, 4)), device_id_type=MESH,
        )

    here = pltpu.make_async_copy(cst, cz.at[pair], jsem.at[4 + pair])
    for e in (2, 1, 3):
        cond_copy(e).start()

    @pl.when(owner)
    def _():
        here.start()

    @pl.when(jnp.logical_not(owner))
    def _():
        cond_copy(0).start()

    y_wu = send(half(w_up, 1 - yh), own_u, pdev(4))
    au = to_neighbours(half(w_up, yh), own_u)
    for c, d in zip(x_wm, (0,) + far):
        arrive([c])
        if d > 0:
            arrive([r_wm[far.index(d)]])
        pd = lax.rem(p + 8 - d, 8)
        wm[pd] = jnp.concatenate(
            [wmx[0, pd].astype(F32), wmx[1, pd].astype(F32)], axis=0
        ).astype(BF16)
    du = hand_over(wu, yh, au)
    for j in range(4):
        pltpu.make_async_copy(cst, cz.at[j], jsem.at[4 + j]).wait()

    wmod = wm[...].reshape(384, 1152)
    pooled = cz[...].reshape(128, 384)
    mps[...] = dot_nn(pooled, wmod[:, :768]).astype(BF16).reshape(4, rows, 768)
    r_mr, r_mg = [], []
    for d in (2, 1, 3):
        dev = zdev(2 * d)
        r_mr.append(send(mps.at[dev[1] // 2], mrs.at[d - 1], dev))
    mpg[...] = dot_nn(pooled, wmod[:, 768:]).astype(BF16).reshape(4, rows, 384)
    for d in (2, 1, 3):
        dev = zdev(2 * d)
        r_mg.append(send(mpg.at[dev[1] // 2], mrg.at[d - 1], dev))
    arrive([y_wu])
    y_wd = send(half(w_down, 1 - yh), own_d, pdev(4))
    cu = to_neighbours(oth_u, oth_u)
    ad = to_neighbours(half(w_down, yh), own_d)

    def to_group(which, val):
        slot[which] = dot_nn(onehot, val).astype(BF16).reshape(8, 16, 384)
        hd[which, m, pl.ds(0, 16)] = slot[which, z]
        out = []
        for d in (4, 3, 5, 2, 6, 1, 7):
            dev = zdev(d)
            out.append(send(slot.at[which, dev[1]], hd.at[which, m, pl.ds(16 * d, 16)], dev))
        return out

    mod = mps[pair].astype(F32)
    arrive(r_mr)
    for d in range(3):
        mod = mod + mrs[d].astype(F32)
    r_sh = to_group(0, (normed * (1.0 + mod[:, 384:]) + mod[:, :384]).astype(BF16))
    gate = mpg[pair].astype(F32)
    arrive(r_mg)
    for d in range(3):
        gate = gate + mrg[d].astype(F32)
    r_sd = to_group(1, (gate * cot).astype(BF16))

    first, second = [], []
    for which, got in ((0, r_sh), (1, r_sd)):
        arrive(got)
        here_rows = hd.at[which, m]
        first.append([send(here_rows, here_rows, ydev(d)) for d in (2, 1, 3)])
        second.append([send(here_rows, here_rows, twin)])
        if which == 0:
            eu = hand_over(wu, 1 - yh, cu)
    arrive([y_wd])
    cd = to_neighbours(oth_d, oth_d)
    dd = hand_over(wd, yh, ad)
    r_pk += [send(pick, pkg.at[par * 4 + pair], zdev(d)) for d in (4, 3, 5, 2, 6)]

    def hand_on(which):
        for c, d in zip(first[which], (2, 1, 3)):
            arrive([c])
            k = 2 * lax.rem(ypos + 4 - d, 4) + core
            second[which].append(send(hd.at[which, k], hd.at[which, k], twin))

    hand_on(0)
    arrive(second[0])
    c_wu.wait()
    arrive(du + eu)

    def both(which, k):
        return jnp.concatenate([hd[which, k], hd[which, 4 + k]], axis=0)

    def reduce_out(val, weight, out, sib, whole, got):
        for k in range(4):
            res = dot_nt(val, weight[384 * k : 384 * k + 384, :]).astype(BF16)
            out[k % 2, k // 2] = res[:128]
            out[k % 2, 2 + k // 2] = res[128:]
        return [
            send(out.at[1 - core, yplace(d)], sib.at[yplace(d)], twin) for d in (2, 1, 3, 0)
        ]

    def reduce_chips(ex, out, sib, whole, got):
        sends = []
        for c, d in zip(ex, (2, 1, 3, 0)):
            arrive([c])
            k = yplace(d)
            whole[k] = (out[core, k].astype(F32) + sib[k].astype(F32)).astype(BF16)
            if d > 0:
                sends.append(send(whole.at[k], got.at[d - 1], ydev(d)))
        return sends

    def reduce_end(ex, whole, got):
        arrive(ex)
        res = whole[ypos].astype(F32)
        for d in range(3):
            res = res + got[d].astype(F32)
        return res.astype(BF16).reshape(8, 16, 384)

    pre = dot_nn(both(0, 0), wu[0:384, :])
    for k in range(1, 4):
        pre = pre + dot_nn(both(0, k), wu[384 * k : 384 * k + 384, :])
    value, slope = gelu_pair(pre)
    act = value.astype(BF16)
    slope_s[...] = slope
    hand_on(1)
    c_wd.wait()
    ed = hand_over(wd, 1 - yh, cd)
    arrive(dd + ed)
    ff_ex = reduce_out(act, wd, ffs, fsib, fsum, rff)
    arrive(second[1])
    d_act = dot_nn(both(1, 0), wd[0:384, :])
    for k in range(1, 4):
        d_act = d_act + dot_nn(both(1, k), wd[384 * k : 384 * k + 384, :])
    d_pre = (d_act * slope_s[...]).astype(BF16)
    r_ff = reduce_chips(ff_ex, ffs, fsib, fsum, rff)
    dh_ex = reduce_out(d_pre, wu, dhs, dsib, dsum, rdh)
    r_dh = reduce_chips(dh_ex, dhs, dsib, dsum, rdh)
    rets[0] = reduce_end(r_ff, fsum, rff)
    r_rt = [send(rets.at[0, d], ret.at[0, z], zdev(-d)) for d in (4, 3, 5, 2, 6, 1, 7)]
    ret[0, z] = rets[0, 0]
    rets[1] = reduce_end(r_dh, dsum, rdh)
    r_rd = [send(rets.at[1, d], ret.at[1, z], zdev(-d)) for d in (4, 3, 5, 2, 6, 1, 7)]
    ret[1, z] = rets[1, 0]
    arrive(r_rt)
    ff_out = dot_nn(onehot_f, ret[0].reshape(128, 384))
    rdm2[pair] = (valid * (cot * ff_out)).astype(BF16)
    r_dm = [send(rdm2.at[pair], rdm2.at[pair], zdev(2 * d)) for d in (2, 1, 3)]
    gen_o[...] = (valid * (lat_t + gate * ff_out)).reshape(4, 8, 384).astype(BF16)
    arrive(r_rd)
    d_hin = dot_nn(onehot_f, ret[1].reshape(128, 384))
    rdm[pair] = jnp.concatenate([valid * d_hin, valid * (d_hin * normed)], axis=1).astype(BF16)
    r_dn = [send(rdm.at[pair], rdm.at[pair], zdev(2 * d)) for d in (2, 1, 3)]
    arrive(r_dm)
    wmod = wm[...].reshape(384, 1152)
    dc_part = dot_nt(rdm2[...].reshape(128, 384), wmod[:, 768:])
    arrive(r_dn)
    dc_part = dc_part + dot_nt(rdm[...].reshape(128, 768), wmod[:, :768])
    turned = dc_part.T
    for h in range(2):
        dcs[h] = jnp.concatenate(
            [turned[48 * pp + 24 * h : 48 * pp + 24 * h + 24] for pp in range(8)], axis=0
        ).astype(BF16)

    def over_tp(h):
        return [send(dcs.at[h], dcr.at[h, e - 1], tdev(e)) for e in (2, 3, 1)]

    def summed(h, copies):
        arrive(copies)
        res = dcs[h].astype(F32)
        for e in range(3):
            res = res + dcr[h, e].astype(F32)
        dcx[h] = res.astype(BF16)

    r_d1 = over_tp(1 - par)
    r_d0 = over_tp(par)
    summed(1 - par, r_d1)
    r_df = [send(dcx.at[1 - par], dcf.at[par], partner)]
    summed(par, r_d0)
    dcf[par] = dcx[par]
    d_cond = jnp.concatenate([dcx[0].astype(F32), dcx[1].astype(F32)], axis=0).T
    dcz[...] = d_cond.astype(BF16).reshape(4, rows, 384)
    r_dz = []
    for d in (2, 1, 3):
        dev = zdev(2 * d)
        r_dz.append(send(dcz.at[dev[1] // 2], dch.at[pair], dev))
    dch[pair] = dcz[pair]

    arrive(r_pk)
    arrive(r_df)
    r_cg = []
    for h in range(2):
        sides = []
        for i in range(2):
            cols = pl.ds(1024 * h + 512 * i, 512)
            res = dot_nn(dcf[0], pkg[0:4, :, cols].reshape(128, 512))
            res = res + dot_nn(dcf[1], pkg[4:8, :, cols].reshape(128, 512))
            sides.append(res.reshape(8, 24, 512))
        cgs[h] = jnp.concatenate(
            [sides[0][:, :16], sides[1][:, :16], sides[0][:, 16:24], sides[1][:, 16:24]], axis=1
        ).astype(BF16)
        for d in (4, 2, 6, 1, 7, 3, 5):
            dev = pdev(d)
            r_cg.append(send(cgs.at[h, dev[0]], rcg.at[h, d - 1], dev))

    arrive(r_dz)
    back = jnp.concatenate([dch[q].astype(F32) for q in range(4)], axis=1).T
    pieces = []
    for pp in range(8):
        for q in range(4):
            for h in range(2):
                k = 384 * q + 192 * h + 24 * pp
                pieces.append(back[k : k + 24])
    back = jnp.concatenate(pieces, axis=0).T.astype(BF16)
    for i in range(4):
        cols = pl.ds(512 * i, 512)
        row_o[:, :, cols] = dot_nn(back, wc[:, cols]).reshape(4, 8, 512).astype(BF16)

    for h in range(2):
        arrive(r_cg[7 * h : 7 * h + 7])
        cg = cgs[h, p].astype(F32)
        for e in range(7):
            cg = cg + rcg[h, e].astype(F32)
        cg = cg * (1.0 / 64.0)
        for i in range(2):
            cols = pl.ds(1024 * h + 512 * i, 512)
            conn_o[0:16, cols] = cg[16 * i : 16 * i + 16]
            conn_o[16:24, cols] = cg[32 + 8 * i : 40 + 8 * i]
    for c in sent:
        c.wait_send()
    for e in range(1, 4):
        cond_copy(e).wait_send()

    @pl.when(jnp.logical_not(owner))
    def _():
        cond_copy(0).wait_send()


def hand_out(gen, row, conn, gen_o, row_o, conn_o):
    gen_o[...] = gen[...]
    row_o[...] = row[...]
    conn_o[...] = conn[...]


def local(hidden, positions, image_tokens, groups, latents, out_grad, w_conn, w_mod, w_up, w_down):
    vm = pl.BlockSpec(memory_space=pltpu.VMEM)
    sm = pl.BlockSpec(memory_space=pltpu.SMEM)
    hb = pl.BlockSpec(memory_space=pl.ANY)
    V = pltpu.VMEM
    n_copies = 200
    outs = pl.pallas_call(
        kernel,
        out_shape=(
            jax.ShapeDtypeStruct((4, 8, 384), BF16),
            jax.ShapeDtypeStruct((4, 8, 2048), BF16),
            jax.ShapeDtypeStruct((24, 2048), F32),
        ),
        in_specs=[sm, sm, sm, hb, hb, hb, hb, hb, hb, hb],
        out_specs=(vm, vm, vm),
        scratch_shapes=[
            V((4, 128, 2048), BF16),
            V((4, 8, 1536), BF16),
            V((4, 8, 384), BF16),
            V((3, 24, 384), BF16),
            V((1536, 2048), BF16),
            V((1536, 768), BF16),
            V((1536, 768), BF16),
            V((2, 8, 24, 1152), BF16),
            V((8, 48, 1152), BF16),
            V((32, 2048), BF16),
            V((8, 32, 2048), BF16),
            V((4, 32, 384), BF16),
            V((3, 32, 384), BF16),
            V((32, 384), BF16),
            V((4, 32, 384), BF16),
            V((4, 32, 768), BF16),
            V((3, 32, 768), BF16),
            V((4, 32, 384), BF16),
            V((3, 32, 384), BF16),
            V((2, 8, 16, 384), BF16),
            V((2, 8, 128, 384), BF16),
            V((256, 768), F32),
            V((2, 4, 128, 384), BF16),
            V((4, 128, 384), BF16),
            V((4, 128, 384), BF16),
            V((3, 128, 384), BF16),
            V((2, 4, 128, 384), BF16),
            V((4, 128, 384), BF16),
            V((4, 128, 384), BF16),
            V((3, 128, 384), BF16),
            V((2, 8, 16, 384), BF16),
            V((2, 8, 16, 384), BF16),
            V((4, 32, 768), BF16),
            V((4, 32, 384), BF16),
            V((2, 192, 128), BF16),
            V((2, 3, 192, 128), BF16),
            V((4, 32, 384), BF16),
            V((2, 192, 128), BF16),
            V((2, 192, 128), BF16),
            V((4, 32, 384), BF16),
            V((2, 8, 48, 512), BF16),
            V((2, 7, 48, 512), BF16),
            pltpu.SemaphoreType.DMA((12,)),
            pltpu.SemaphoreType.DMA((n_copies,)),
            pltpu.SemaphoreType.DMA((n_copies,)),
            pltpu.SemaphoreType.DMA((8,)),
        ],
        compiler_params=pltpu.CompilerParams(
            collective_id=0, has_side_effects=True, vmem_limit_bytes=56 * 2**20
        ),
        cost_estimate=pl.CostEstimate(
            flops=6_000_000_000, bytes_accessed=16_000_000, transcendentals=200_000
        ),
    )(
        groups.reshape(4), image_tokens, positions, hidden, latents, out_grad, w_conn,
        jnp.transpose(w_mod, (1, 0, 2)), w_up, w_down,
    )
    return pl.pallas_call(
        hand_out,
        out_shape=tuple(jax.ShapeDtypeStruct(o.shape, o.dtype) for o in outs),
        in_specs=[vm, vm, vm],
        out_specs=(vm, vm, vm),
    )(*outs)


def solution(mesh):
    placed = (
        P(("pp", "dp"), None, "tp"),
        P(("pp", "dp"), None),
        P(("pp", "dp")),
        P(("pp", "dp"), None),
        P(("pp", "dp"), None, None),
        P(("pp", "dp"), None, "tp"),
        P(None, "tp"),
        P(("pp", "dp"), None, "tp"),
        P("dp", "pp", "tp"),
        P("dp", "pp", "tp"),
    )
    return jax.shard_map(
        local,
        mesh=mesh,
        in_specs=placed,
        out_specs=(P(("pp", "dp"), None, "tp"), P(("pp", "dp"), None, "tp"), P(("pp", "dp"), "tp")),
        check_vma=False,
    )
```
